32 devices in a mesh: section: 2 (over x), row: 4 (over y, core), col: 4 (over z).
Axes of the slice: x: 2, y: 2, z: 4, core: 2. Of those that a mesh axis runs over, the one named last changes fastest.
Arguments:
- image: bfloat16 [32, 64, 1024], P('section', 'row', 'col'), may hold values from -6 to 6
- conv_kernel: float32 [7, 7, 1024], P(None, None, 'col'), may hold values from -0.875 to 0.875
- norm_gain: float32 [1024], P('col'), may hold values from 0.1 to 1.9
- w_in: bfloat16 [1024, 4096], P('row', 'col'), may hold values from -0.1875 to 0.1875
- w_out: bfloat16 [4096, 1024], P('row', 'col'), may hold values from -0.09375 to 0.09375
- upstream: bfloat16 [32, 64, 1024], P('section', 'row', 'col'), may hold values from -6 to 6
Outputs:
- output: bfloat16 [32, 64, 1024], P('section', 'row', 'col')
- image_grad: float32 [32, 64, 1024], P('section', 'row', 'col')
The draws below stay inside these ranges and needn't reach their ends.
All inputs are finite; a program needn't handle non-finite values.
Results may differ from the reference program's by a relative error of at most 0.0095.
Values may be sent and summed in bfloat16 or wider, within the bound.
No kernel may reach another device: no remote copies, remote signals or barrier semaphores. Data moves between devices by JAX's collectives and lax.ppermute only.
A program may use at most 64 MiB of HBM per device.

```python
import math
import jax
import jax.numpy as jnp
from jax import lax

C = 1024
HID = 4096
KERNEL = 7
NLAT = 32
NLON = 64
N_COL = 4


def levels(rng, shape, shards, smallest, high):
    gain, own = 1.0, jax.random.fold_in(rng, 6)
    for axis_at, shards_of in shards:
        steps = jnp.exp(jax.random.uniform(jax.random.fold_in(own, axis_at), (shards_of,), jnp.float32, smallest / len(shards), high / len(shards)))
        gain = gain * jnp.repeat(steps, shape[axis_at] // shards_of).reshape([-1 if axis == axis_at else 1 for axis in range(len(shape))])
    return gain


def normal_values(own_key, shape, scale, bound, pieces=(), held_as=jnp.bfloat16):
    drawn = jax.random.normal(own_key, shape, jnp.float32) * scale
    if len(pieces) > 0:
        drawn = levels(own_key, shape, pieces, -0.22, 0.18) * drawn
    return jnp.clip(drawn, min=-bound, max=bound).astype(held_as)


def setup_inputs(seed: int = 0) -> dict:
    keys = jax.random.split(jax.random.key(seed), 7)
    return {
        "image": normal_values(keys[0], (NLAT, NLON, C), 1.0, 6.0, ((0, 2), (1, 4), (2, 4))),
        "conv_kernel": normal_values(keys[1], (KERNEL, KERNEL, C), (KERNEL * KERNEL) ** -0.5, 0.875, ((2, 4),), jnp.float32),
        "norm_gain": jnp.clip(1.0 + 0.18 * jax.random.normal(keys[2], (C,), jnp.float32), 0.1, 1.9),
        "w_in": normal_values(keys[3], (C, HID), C ** -0.5, 0.1875, ((0, 4), (1, 4))),
        "w_out": normal_values(keys[4], (HID, C), HID ** -0.5, 0.09375, ((0, 4), (1, 4))),
        "upstream": normal_values(keys[5], (NLAT, NLON, C), 1.0, 6.0, ((0, 2), (1, 4), (2, 4))),
    }


EPSILON = 1e-06

def depthwise(padded, kernel, height, breadth, start):
    total = jnp.zeros((height, breadth, padded.shape[2]), jnp.float32)
    for row_off in range(KERNEL):
        for col_off in range(KERNEL):
            lead = start - row_off if start > 0 else row_off
            side = start - col_off if start > 0 else col_off
            total = total + padded[lead:lead + height, side:side + breadth, :] * kernel[row_off, col_off]
    return total

def gelu_slope(preact):
    return 0.5 * (1.0 + lax.erf(preact / math.sqrt(2.0))) + preact * jnp.exp(-0.5 * preact * preact) / math.sqrt(2.0 * math.pi)

def reference(image, conv_kernel, norm_gain, w_in, w_out, upstream):
    height, breadth, channels = image.shape
    margin = KERNEL // 2
    widths = ((margin, margin), (margin, margin), (0, 0))
    mixed = depthwise(jnp.pad(image.astype(jnp.float32), widths), conv_kernel, height, breadth, 0)
    centre = lax.optimization_barrier(jnp.mean(mixed, axis=-1, keepdims=True))
    centred = mixed - centre
    spread = lax.optimization_barrier(jnp.mean(centred * centred, axis=-1, keepdims=True))
    inv_std = lax.rsqrt(spread + EPSILON)
    normed = centred * inv_std
    scaled = (normed * norm_gain).astype(jnp.bfloat16).reshape(-1, channels)
    preact = jnp.dot(scaled, w_in, preferred_element_type=jnp.float32)
    hidden = jax.nn.gelu(preact, approximate=False).astype(jnp.bfloat16)
    branch = jnp.dot(hidden, w_out, preferred_element_type=jnp.float32)
    flat_image = image.reshape(-1, channels).astype(jnp.float32)
    output = (flat_image + branch).astype(jnp.bfloat16).reshape(image.shape)
    grad_flat = upstream.reshape(-1, channels)
    chan_block = channels // N_COL
    hid_block = w_in.shape[1] // N_COL
    hidden_grad = jnp.zeros(preact.shape, jnp.float32)
    for block in range(N_COL):
        lo_c = block * chan_block
        term = jnp.dot(grad_flat[:, lo_c:lo_c + chan_block], w_out[:, lo_c:lo_c + chan_block].T, preferred_element_type=jnp.float32)
        term = lax.optimization_barrier(term.astype(jnp.bfloat16))
        hidden_grad = hidden_grad + term.astype(jnp.float32)
    act_grad = (hidden_grad * gelu_slope(preact)).astype(jnp.bfloat16)
    feature_grad = jnp.zeros(scaled.shape, jnp.float32)
    for block in range(N_COL):
        lo_h = block * hid_block
        term = jnp.dot(act_grad[:, lo_h:lo_h + hid_block], w_in[:, lo_h:lo_h + hid_block].T, preferred_element_type=jnp.float32)
        term = lax.optimization_barrier(term.astype(jnp.bfloat16))
        feature_grad = feature_grad + term.astype(jnp.float32)
    normed_grad = feature_grad.reshape(image.shape) * norm_gain
    first = lax.optimization_barrier(jnp.mean(normed_grad, axis=-1, keepdims=True))
    second = lax.optimization_barrier(jnp.mean(normed_grad * normed, axis=-1, keepdims=True))
    mixed_grad = inv_std * (normed_grad - first - normed * second)
    grad_pad = jnp.pad(mixed_grad, widths)
    image_grad = upstream.astype(jnp.float32) + depthwise(grad_pad, conv_kernel, height, breadth, 2 * margin)
    return (output, image_grad)
```

```python
import functools
import math

import jax
import jax.numpy as jnp
from jax import lax
from jax.experimental import pallas as pl
from jax.experimental.pallas import tpu as pltpu
from jax.sharding import PartitionSpec as P

KERNEL = 7
MARGIN = KERNEL // 2
EPSILON = 1e-06
BF16, F32 = jnp.bfloat16, jnp.float32
VMEM_LIMIT = 40 * 1024 * 1024


def round_up(value, to):
    return -(-value // to) * to


def bits_of(count):
    return [1 << b for b in range(count.bit_length() - 1)]


def swap(x, axis, bit):
    count = lax.axis_size(axis)
    return lax.ppermute(x, axis, [(i, i ^ bit) for i in range(count)])


def pairings(count):
    both = [
        [(i, i + 1) for i in range(first, count - 1, 2)] for first in range(2)
    ]
    return [p + [(b, a) for a, b in p] for p in both if p]


def faces_up(index, pairing):
    return (index + pairing) % 2 == 0


def halo_kinds(n_sec, n_row):
    secs, rows = range(len(pairings(n_sec))), range(len(pairings(n_row)))
    return (
        [(a, None) for a in secs]
        + [(None, b) for b in rows]
        + [(a, b) for a in secs for b in rows]
    )


def halo_rows(kind, height, breadth):
    if kind[1] is None:
        return MARGIN * breadth
    if kind[0] is None:
        return MARGIN * height
    return round_up(MARGIN * MARGIN, 16)


def halo_permute(strip, kind, n_sec, n_row):
    secs, rows = pairings(n_sec), pairings(n_row)
    if kind[1] is None:
        return lax.ppermute(strip, "section", secs[kind[0]])
    if kind[0] is None:
        return lax.ppermute(strip, "row", rows[kind[1]])
    pairs = [
        (a * n_row + c, b * n_row + d)
        for a, b in secs[kind[0]]
        for c, d in rows[kind[1]]
    ]
    return lax.ppermute(strip, ("section", "row"), pairs)


def emit_strips(cells, corner, outs, kinds, height, breadth):
    sec, row = lax.axis_index("section"), lax.axis_index("row")
    for lane in range(cells.shape[0]):
        block, lanes = cells.at[lane], slice(lane * 128, (lane + 1) * 128)
        for out, (a, b) in zip(outs, kinds):
            if b is None:
                up = faces_up(sec, a)
                size = MARGIN * breadth
                out[:, lanes] = jnp.where(
                    up, block[height * breadth - size :, :], block[:size, :]
                ).astype(BF16)
            elif a is None:
                up = faces_up(row, b)
                for j in range(MARGIN):
                    out[j * height : (j + 1) * height, lanes] = jnp.where(
                        up,
                        block[pl.ds(breadth - MARGIN + j, height, stride=breadth), :],
                        block[pl.ds(j, height, stride=breadth), :],
                    ).astype(BF16)
            else:
                up, right = faces_up(sec, a), faces_up(row, b)
                corner[...] = jnp.zeros_like(corner)
                for i in range(MARGIN):
                    sides = []
                    for start in ((height - MARGIN + i) * breadth, i * breadth):
                        sides.append(
                            jnp.where(
                                right,
                                block[start + breadth - MARGIN : start + breadth, :],
                                block[start : start + MARGIN, :],
                            )
                        )
                    corner[i * MARGIN : (i + 1) * MARGIN, :] = jnp.where(up, *sides)
                out[:, lanes] = corner[...].astype(BF16)


def low_high(index, received):
    if not received:
        return None, None
    first = received[0]
    second = received[1] if len(received) > 1 else jnp.zeros_like(first)
    odd = index % 2 == 1
    return jnp.where(odd, first, second), jnp.where(odd, second, first)


LEFT = 8


def padded_width(breadth):
    return round_up(LEFT + breadth + MARGIN, 8)


def fill_padded(pad, cells, halos, kinds, height, breadth):
    sec, row = lax.axis_index("section"), lax.axis_index("row")
    width = padded_width(breadth)
    got = dict(zip(kinds, halos))
    secs = sorted({a for a, b in kinds if b is None})
    rows = sorted({b for a, b in kinds if a is None})
    for lane in range(pad.shape[0]):
        block, lanes = pad.at[lane], slice(lane * 128, (lane + 1) * 128)

        def arrived(*kind):
            return got[kind][:, lanes].astype(F32)

        block[: MARGIN * width, :] = jnp.zeros((MARGIN * width, 128), F32)
        block[(MARGIN + height) * width :, :] = jnp.zeros((MARGIN * width, 128), F32)
        for i in range(height):
            start = (MARGIN + i) * width + LEFT
            block[start : start + breadth, :] = cells[i * breadth : (i + 1) * breadth, lanes].astype(F32)
        low, high = low_high(sec, [arrived(a, None) for a in secs])
        if low is not None:
            for i in range(MARGIN):
                for top, strip in ((i, low), (MARGIN + height + i, high)):
                    start = top * width + LEFT
                    block[start : start + breadth, :] = strip[i * breadth : (i + 1) * breadth, :]
        low, high = low_high(row, [arrived(None, b) for b in rows])
        for j in range(MARGIN):
            for column, strip in ((LEFT - MARGIN + j, low), (LEFT + breadth + j, high)):
                block[pl.ds(MARGIN * width + column, height, stride=width), :] = (
                    jnp.zeros((height, 128), F32)
                    if strip is None
                    else strip[j * height : (j + 1) * height, :]
                )
        if secs and rows:
            by_sec = [low_high(row, [arrived(a, b) for b in rows]) for a in secs]
            for column, k in ((LEFT - MARGIN, 0), (LEFT + breadth, 1)):
                low, high = low_high(sec, [pair[k] for pair in by_sec])
                for i in range(MARGIN):
                    for top, strip in ((i, low), (MARGIN + height + i, high)):
                        start = top * width + column
                        block[start : start + MARGIN, :] = strip[i * MARGIN : (i + 1) * MARGIN, :]


def convolve(pad, shifted, taps, height, breadth, flip, store):
    width = padded_width(breadth)
    tall = height + 2 * MARGIN
    step = 4 if height % 4 == 0 else 1
    for lane in range(pad.shape[0]):
        lanes = slice(lane * 128, (lane + 1) * 128)
        for b in range(KERNEL):
            for i in range(tall):
                start = i * width + LEFT - MARGIN + b
                shifted[b, i * breadth : (i + 1) * breadth, :] = pad[lane, start : start + breadth, :]
        for top in range(0, height, step):
            total = jnp.zeros((step * breadth, 128), F32)
            for a in range(KERNEL):
                for b in range(KERNEL):
                    p, q = (KERNEL - 1 - a, KERNEL - 1 - b) if flip else (a, b)
                    first = (top + a) * breadth
                    total += shifted[b, first : first + step * breadth, :] * taps[p, q, lanes][None, :]
            store(slice(top * breadth, (top + step) * breadth), lanes, total)


def strips_kernel(dims, kinds, image, *rest):
    outs, (cells, corner) = rest[: len(kinds)], rest[len(kinds) :]
    for lane in range(cells.shape[0]):
        cells[lane] = image[:, lane * 128 : (lane + 1) * 128].astype(F32)
    emit_strips(cells, corner, outs, kinds, *dims)


def split3(x):
    high = x.astype(BF16)
    left = x - high.astype(F32)
    mid = left.astype(BF16)
    return high, mid, (left - mid.astype(F32)).astype(BF16)


def message_rows(cells, channels):
    return cells + round_up(2 * (cells // channels) + 3, 16)


def forward_conv_kernel(dims, kinds, image, taps, gain, *rest):
    halos, (message, pad, shifted, mixed, tail) = rest[: len(kinds)], rest[len(kinds) :]
    height, breadth = dims
    cells, channels = image.shape
    fill_padded(pad, image, halos, kinds, height, breadth)

    def store(rows, lanes, total):
        mixed[rows, lanes] = total

    convolve(pad, shifted, taps, height, breadth, False, store)
    mean = jnp.sum(mixed[...], axis=1, keepdims=True) * (1.0 / channels)
    first = mean.astype(BF16).astype(F32)
    second = (mean - first).astype(BF16).astype(F32)
    message[:cells, :] = ((mixed[...] - first) - second).astype(BF16)
    tail[...] = jnp.zeros_like(tail)
    per = cells // channels
    for t, column in enumerate((first, second)):
        flat = jnp.broadcast_to(column, (cells, 128)).T
        for p in range(per):
            tail[t * per + p : t * per + p + 1, :] = flat[:1, p * channels : (p + 1) * channels]
    for t, part in enumerate(split3(gain[...])):
        tail[2 * per + t : 2 * per + t + 1, :] = part.astype(F32)
    message[cells:, :] = tail[...].astype(BF16)


def copy_pieces(pieces, refs, whole, sems):
    copies = []
    for n, (ref, (row_at, column_at)) in enumerate(zip(refs, pieces)):
        rows, columns = ref.shape
        row, column = row_at(), column_at()
        copy = pltpu.make_async_copy(
            ref,
            whole.at[
                pl.ds(row if isinstance(row, int) else pl.multiple_of(row, rows), rows),
                pl.ds(column if isinstance(column, int) else pl.multiple_of(column, columns), columns),
            ],
            sems.at[n],
        )
        copy.start()
        copies.append(copy)
    return copies


def hidden_grad_kernel(pieces, n_col, *refs):
    ups, refs = refs[:n_col], refs[n_col:]
    weights, (out, whole, sems) = refs[: len(pieces)], refs[len(pieces) :]
    copies = copy_pieces(pieces, weights, whole, sems)
    channels = ups[0].shape[1]
    for copy in copies:
        copy.wait()
    hidden = out.shape[1]
    tile = min(512, hidden)
    for start in range(0, hidden, tile):
        total = jnp.zeros((out.shape[0], tile), F32)
        for k in range(n_col):
            total += lax.dot_general(
                ups[k][...],
                whole[start : start + tile, k * channels : (k + 1) * channels],
                (((1,), (1,)), ((), ())),
                preferred_element_type=F32,
            )
        out[:, start : start + tile] = total


def mlp_kernel(pieces, n_col, hidden_grad, *refs):
    messages, refs = refs[:n_col], refs[n_col:]
    weights, refs = refs[: len(pieces)], refs[len(pieces) :]
    outs, refs = refs[:n_col], refs[n_col:]
    hidden, whole, normed, scaled, act_grad, sems = refs
    copies = copy_pieces(pieces, weights, whole, sems)
    cells, channels = outs[0].shape
    all_channels = n_col * channels
    per = cells // channels

    means, gains = [], []
    for message in messages:
        tail = message[cells:, :].astype(F32)
        flat = tail[:per, :] + tail[per : 2 * per, :]
        row = jnp.concatenate([flat[p : p + 1, :] for p in range(per)], axis=1)
        means.append(jnp.broadcast_to(row, (128, cells)).T[:, :1])
        gains.append(tail[2 * per : 2 * per + 1, :] + tail[2 * per + 1 : 2 * per + 2, :] + tail[2 * per + 2 : 2 * per + 3, :])
    centre = sum(means) * (1.0 / n_col)
    spread = jnp.zeros((cells, 1), F32)
    for k, message in enumerate(messages):
        centred = message[:cells, :].astype(F32) + (means[k] - centre)
        normed[k] = centred
        spread += jnp.sum(centred * centred, axis=1, keepdims=True)
    inv_std = lax.rsqrt(spread * (1.0 / all_channels) + EPSILON)
    for k in range(n_col):
        value = normed[k] * inv_std
        normed[k] = value
        scaled[:, k * channels : (k + 1) * channels] = (value * gains[k]).astype(BF16)
    for copy in copies:
        copy.wait()
    width = hidden.shape[1]
    tile = min(256, width)
    for start in range(0, width, tile):
        preact = jnp.dot(scaled[...], whole[:, start : start + tile], preferred_element_type=F32)
        phi = 0.5 * (1.0 + lax.erf(preact * math.sqrt(0.5)))
        hidden[:, start : start + tile] = (preact * phi).astype(BF16)
        slope = phi + preact * jnp.exp(-0.5 * preact * preact) * (1.0 / math.sqrt(2.0 * math.pi))
        act_grad[:, start : start + tile] = (hidden_grad[:, start : start + tile] * slope).astype(BF16)
    first, second = jnp.zeros((cells, 1), F32), jnp.zeros((cells, 1), F32)
    grads = []
    for k in range(n_col):
        grad = lax.dot_general(
            act_grad[...],
            whole[k * channels : (k + 1) * channels, :],
            (((1,), (1,)), ((), ())),
            preferred_element_type=F32,
        ) * gains[k]
        grads.append(grad)
        first += jnp.sum(grad, axis=1, keepdims=True)
        second += jnp.sum(grad * normed[k], axis=1, keepdims=True)
    first, second = first * (1.0 / all_channels), second * (1.0 / all_channels)
    for k in range(n_col):
        outs[k][...] = (inv_std * (grads[k] - first - normed[k] * second)).astype(BF16)


def branch_kernel(pieces, n_col, hidden, *refs):
    weights, refs = refs[: len(pieces)], refs[len(pieces) :]
    outs, (whole, sems) = refs[:n_col], refs[n_col:]
    copies = copy_pieces(pieces, weights, whole, sems)
    channels = outs[0].shape[1]
    for copy in copies:
        copy.wait()
    for k in range(n_col):
        outs[k][...] = jnp.dot(
            hidden[...], whole[:, k * channels : (k + 1) * channels], preferred_element_type=F32
        ).astype(BF16)


def grad_sum_kernel(dims, kinds, n_col, *refs):
    parts, refs = refs[:n_col], refs[n_col:]
    total, refs = refs[0], refs[1:]
    outs, (blocks, corner) = refs[: len(kinds)], refs[len(kinds) :]
    for lane in range(blocks.shape[0]):
        lanes = slice(lane * 128, (lane + 1) * 128)
        blocks[lane] = sum(part[:, lanes].astype(F32) for part in parts)
        total[:, lanes] = blocks[lane]
    emit_strips(blocks, corner, outs, kinds, *dims)


def backward_conv_kernel(dims, kinds, grad, taps, upstream, *rest):
    halos, (out, pad, shifted) = rest[: len(kinds)], rest[len(kinds) :]
    height, breadth = dims
    fill_padded(pad, grad, halos, kinds, height, breadth)

    def store(rows, lanes, total):
        out[rows, lanes] = total + upstream[rows, lanes].astype(F32)

    convolve(pad, shifted, taps, height, breadth, True, store)


def call(kernel, out_shape, in_specs, scratch, flops=0, bytes_accessed=1 << 20, transcendentals=0):
    return pl.pallas_call(
        kernel,
        out_shape=out_shape,
        in_specs=in_specs,
        out_specs=jax.tree.map(lambda _: pl.BlockSpec(memory_space=pltpu.VMEM), out_shape),
        scratch_shapes=scratch,
        compiler_params=pltpu.CompilerParams(vmem_limit_bytes=VMEM_LIMIT),
        cost_estimate=pl.CostEstimate(
            flops=flops, bytes_accessed=bytes_accessed, transcendentals=transcendentals
        ),
    )


IN_VMEM = pl.BlockSpec(memory_space=pltpu.VMEM)
ANYWHERE = pl.BlockSpec(memory_space=pl.ANY)


def spread_weights(w_in, w_out):
    n_sec, n_row, n_col = (lax.axis_size(a) for a in ("section", "row", "col"))
    channels, hidden = w_in.shape[0] * n_row // n_col, w_in.shape[1]
    if n_row != n_col or n_row & (n_row - 1) or n_sec & (n_sec - 1):
        order = jnp.arange(n_col) ^ lax.axis_index("col")
        whole_in = lax.all_gather(w_in, "row", axis=0, tiled=True)
        whole_in = whole_in.reshape(n_col, channels, hidden)[order].reshape(-1, hidden)
        whole_out = lax.all_gather(w_out, "row", axis=0, tiled=True)
        whole_out = lax.all_to_all(whole_out, "col", 0, 1, tiled=True)
        whole_out = whole_out.reshape(hidden, n_col, channels)[:, order].reshape(hidden, -1)
        none = (lambda: 0, lambda: 0)
        return [whole_in], [none], [whole_out], [none]

    section = lax.axis_index("section")
    share = hidden // n_sec

    def place(row_bits, sec_bits):
        block = lambda: ((lax.axis_index("row") ^ row_bits) ^ lax.axis_index("col")) * channels
        part = (lambda: 0) if sec_bits is None else (lambda: (lax.axis_index("section") ^ sec_bits) * share)
        return block, part

    mine_out = lax.dynamic_slice_in_dim(w_out, section * share, share, 0)
    mine_out = lax.ppermute(
        mine_out,
        ("row", "col"),
        [(r * n_col + z, z * n_col + r) for r in range(n_row) for z in range(n_col)],
    )
    far = [b for b in bits_of(n_row) if b > 1]
    mine_in = lax.dynamic_slice_in_dim(w_in, section * share, share, 1)

    def spread(piece, keep):
        got = {(0, 0): piece}
        for bit in far:
            got |= {(r ^ bit, s): swap(x, "row", bit) for (r, s), x in got.items()}
        for bit in bits_of(n_sec):
            got |= {
                (r, s ^ bit): swap(x, "section", bit)
                for (r, s), x in got.items()
                if keep or r > 0
            }
        return got

    got_in = {k: x for k, x in spread(mine_in, False).items() if k[0] > 0}
    got_in[0, None] = w_in
    got_out = spread(mine_out, True)
    for got in (got_in, got_out):
        for bit in bits_of(n_row)[:1]:
            got |= {(r ^ bit, s): swap(x, "row", bit) for (r, s), x in got.items()}
    return (
        list(got_in.values()),
        [place(*k) for k in got_in],
        list(got_out.values()),
        [place(*k)[::-1] for k in got_out],
    )


def local(image, conv_kernel, norm_gain, w_in, w_out, upstream):
    height, breadth, channels = image.shape
    dims = (height, breadth)
    cells = height * breadth
    n_sec, n_row, n_col = (lax.axis_size(a) for a in ("section", "row", "col"))
    all_channels, hidden = n_col * channels, w_in.shape[1]
    kinds = halo_kinds(n_sec, n_row)
    strips = [
        jax.ShapeDtypeStruct((halo_rows(k, height, breadth), channels), BF16) for k in kinds
    ]
    corner = pltpu.VMEM((round_up(MARGIN * MARGIN, 16), 128), F32)
    blocks = pltpu.VMEM((channels // 128, cells, 128), F32)
    padded = [
        pltpu.VMEM((channels // 128, (height + 2 * MARGIN) * padded_width(breadth), 128), F32),
        pltpu.VMEM((KERNEL, (height + 2 * MARGIN) * breadth, 128), F32),
    ]
    conv_cost = dict(flops=2 * KERNEL * KERNEL * cells * channels * 30)

    def exchange(sent):
        return [halo_permute(s, k, n_sec, n_row) for s, k in zip(sent, kinds)]

    def to_col(parts):
        return [p if k == 0 else swap(p, "col", k) for k, p in enumerate(parts)]

    flat_image = image.reshape(cells, channels)
    flat_up = upstream.reshape(cells, channels)
    sent = call(
        functools.partial(strips_kernel, dims, kinds),
        strips,
        [IN_VMEM],
        [blocks, corner],
    )(flat_image)
    halos = exchange(sent)
    in_refs, in_pieces, out_refs, out_pieces = spread_weights(w_in, w_out)
    ups = to_col([flat_up] * n_col)
    rows = message_rows(cells, channels)
    message = call(
        functools.partial(forward_conv_kernel, dims, kinds),
        jax.ShapeDtypeStruct((rows, channels), BF16),
        [IN_VMEM] * (3 + len(kinds)),
        padded + [pltpu.VMEM((cells, channels), F32), pltpu.VMEM((rows - cells, channels), F32)],
        **conv_cost,
    )(flat_image, conv_kernel, norm_gain.reshape(1, channels), *halos)
    messages = to_col([message] * n_col)

    product = 2 * cells * all_channels * hidden
    weight = pltpu.VMEM((all_channels, hidden), BF16)
    weight_t = pltpu.VMEM((hidden, all_channels), BF16)
    hidden_grad = call(
        functools.partial(hidden_grad_kernel, out_pieces, n_col),
        jax.ShapeDtypeStruct((cells, hidden), F32),
        [IN_VMEM] * n_col + [ANYWHERE] * len(out_refs),
        [weight_t, pltpu.SemaphoreType.DMA((len(out_refs),))],
        flops=product,
    )(*ups, *out_refs)
    part = jax.ShapeDtypeStruct((cells, channels), BF16)
    *grads, act = call(
        functools.partial(mlp_kernel, in_pieces, n_col),
        [part] * n_col + [jax.ShapeDtypeStruct((cells, hidden), BF16)],
        [IN_VMEM] * (1 + n_col) + [ANYWHERE] * len(in_refs),
        [
            weight,
            pltpu.VMEM((n_col, cells, channels), F32),
            pltpu.VMEM((cells, all_channels), BF16),
            pltpu.VMEM((cells, hidden), BF16),
            pltpu.SemaphoreType.DMA((len(in_refs),)),
        ],
        flops=2 * product,
        transcendentals=2 * cells * hidden,
    )(hidden_grad, *messages, *in_refs)
    grads = to_col(grads)
    branches = call(
        functools.partial(branch_kernel, out_pieces, n_col),
        [part] * n_col,
        [IN_VMEM] + [ANYWHERE] * len(out_refs),
        [weight_t, pltpu.SemaphoreType.DMA((len(out_refs),))],
        flops=product,
    )(act, *out_refs)
    branches = to_col(branches)
    mixed_grad, *sent = call(
        functools.partial(grad_sum_kernel, dims, kinds, n_col),
        [jax.ShapeDtypeStruct((cells, channels), F32)] + strips,
        [IN_VMEM] * n_col,
        [blocks, corner],
    )(*grads)
    halos = exchange(sent)
    image_grad = call(
        functools.partial(backward_conv_kernel, dims, kinds),
        jax.ShapeDtypeStruct((cells, channels), F32),
        [IN_VMEM] * (3 + len(kinds)),
        padded,
        **conv_cost,
    )(mixed_grad, conv_kernel, flat_up, *halos)
    output = (flat_image.astype(F32) + sum(b.astype(F32) for b in branches)).astype(BF16)
    return output.reshape(image.shape), image_grad.reshape(image.shape)


def solution(mesh):
    in_specs = (
        P("section", "row", "col"),
        P(None, None, "col"),
        P("col"),
        P("row", "col"),
        P("row", "col"),
        P("section", "row", "col"),
    )
    out_specs = (P("section", "row", "col"), P("section", "row", "col"))
    return jax.shard_map(local, mesh=mesh, in_specs=in_specs, out_specs=out_specs, check_vma=False)
```

```python
import functools
import math

import jax
import jax.numpy as jnp
from jax import lax
from jax.experimental import pallas as pl
from jax.experimental.pallas import tpu as pltpu
from jax.sharding import PartitionSpec as P

KERNEL = 7
MARGIN = KERNEL // 2
EPSILON = 1e-06
BF16, F32 = jnp.bfloat16, jnp.float32
MIB = 1024 * 1024


def round_up(value, to):
    return -(-value // to) * to


def bits_of(count):
    return [1 << b for b in range(count.bit_length() - 1)]


def swap(x, axis, bit, name=None):
    count = lax.axis_size(axis)
    with jax.named_scope(name or f"{axis}_{bit}"):
        return lax.ppermute(x, axis, [(i, i ^ bit) for i in range(count)])


def pairings(count):
    both = [[(i, i + 1) for i in range(first, count - 1, 2)] for first in range(2)]
    return [p + [(b, a) for a, b in p] for p in both if p]


def faces_up(index, pairing):
    return (index + pairing) % 2 == 0


def meet(strips, axis, name):
    with jax.named_scope(name):
        return [
            lax.ppermute(strip, axis, pairs)
            for strip, pairs in zip(strips, pairings(lax.axis_size(axis)))
        ]


def low_high(index, received):
    if not received:
        return None, None
    first = received[0]
    second = received[1] if len(received) > 1 else jnp.zeros_like(first)
    odd = index % 2 == 1
    return jnp.where(odd, first, second), jnp.where(odd, second, first)


def side_rows(height):
    return round_up(MARGIN * (height + 2 * MARGIN), 16)


def emit_top(cells, outs, height, breadth):
    size = MARGIN * breadth
    for pairing, out in enumerate(outs):
        up = faces_up(lax.axis_index("section"), pairing)
        for lane in range(cells.shape[0]):
            out[:, lane * 128 : (lane + 1) * 128] = jnp.where(
                up, cells[lane, height * breadth - size :, :], cells[lane, :size, :]
            ).astype(BF16)


def sides_kernel(dims, n_top, cells, *refs):
    height, breadth = dims
    tops, (*outs, blocks) = refs[:n_top], refs[n_top:]
    size = MARGIN * breadth
    tall = height + 2 * MARGIN
    for lane in range(blocks.shape[0]):
        lanes = slice(lane * 128, (lane + 1) * 128)
        block = blocks.at[lane]
        low, high = low_high(lax.axis_index("section"), [top[:, lanes].astype(F32) for top in tops])
        block[:size, :] = jnp.zeros((size, 128), F32) if low is None else low
        block[size : size + height * breadth, :] = cells[:, lanes].astype(F32)
        block[size + height * breadth :, :] = jnp.zeros((size, 128), F32) if high is None else high
        for pairing, out in enumerate(outs):
            up = faces_up(lax.axis_index("row"), pairing)
            columns = [
                jnp.where(
                    up,
                    block[pl.ds(breadth - MARGIN + j, tall, stride=breadth), :],
                    block[pl.ds(j, tall, stride=breadth), :],
                )
                for j in range(MARGIN)
            ]
            spare = out.shape[0] - MARGIN * tall
            if spare:
                columns.append(jnp.zeros((spare, 128), F32))
            out[:, lanes] = jnp.concatenate(columns, axis=0).astype(BF16)


LEFT = 8


def padded_width(breadth):
    return round_up(LEFT + breadth + MARGIN, 8)


def fill_padded(pad, cells, tops, columns, height, breadth):
    width = padded_width(breadth)
    tall = height + 2 * MARGIN
    for lane in range(pad.shape[0]):
        block, lanes = pad.at[lane], slice(lane * 128, (lane + 1) * 128)
        for i in range(height):
            start = (MARGIN + i) * width + LEFT
            block[start : start + breadth, :] = cells[i * breadth : (i + 1) * breadth, lanes].astype(F32)
        low, high = low_high(lax.axis_index("section"), [top[:, lanes].astype(F32) for top in tops])
        for i in range(MARGIN):
            for row, strip in ((i, low), (MARGIN + height + i, high)):
                start = row * width + LEFT
                block[start : start + breadth, :] = (
                    jnp.zeros((breadth, 128), F32)
                    if strip is None
                    else strip[i * breadth : (i + 1) * breadth, :]
                )
        low, high = low_high(lax.axis_index("row"), [c[:, lanes].astype(F32) for c in columns])
        for j in range(MARGIN):
            for column, strip in ((LEFT - MARGIN + j, low), (LEFT + breadth + j, high)):
                block[pl.ds(column, tall, stride=width), :] = (
                    jnp.zeros((tall, 128), F32)
                    if strip is None
                    else strip[j * tall : (j + 1) * tall, :]
                )


def convolve(pad, shifted, taps, height, breadth, flip, store):
    width = padded_width(breadth)
    tall = height + 2 * MARGIN
    step = 4 if height % 4 == 0 else 1
    for lane in range(pad.shape[0]):
        lanes = slice(lane * 128, (lane + 1) * 128)
        for b in range(KERNEL):
            for i in range(tall):
                start = i * width + LEFT - MARGIN + b
                shifted[b, i * breadth : (i + 1) * breadth, :] = pad[lane, start : start + breadth, :]
        for top in range(0, height, step):
            total = jnp.zeros((step * breadth, 128), F32)
            for a in range(KERNEL):
                for b in range(KERNEL):
                    p, q = (KERNEL - 1 - a, KERNEL - 1 - b) if flip else (a, b)
                    first = (top + a) * breadth
                    total += shifted[b, first : first + step * breadth, :] * taps[p, q, lanes][None, :]
            store(slice(top * breadth, (top + step) * breadth), lanes, total)


def split3(x):
    high = x.astype(BF16)
    left = x - high.astype(F32)
    mid = left.astype(BF16)
    return high, mid, (left - mid.astype(F32)).astype(BF16)


def message_rows(cells, channels):
    return 2 * cells + round_up(2 * (cells // channels) + 3, 16)


def forward_conv_kernel(dims, n_top, n_side, image, taps, gain, upstream, *refs):
    tops, columns, refs = refs[:n_top], refs[n_top : n_top + n_side], refs[n_top + n_side :]
    message, pad, shifted, mixed, tail = refs
    height, breadth = dims
    cells, channels = image.shape
    fill_padded(pad, image, tops, columns, height, breadth)

    def store(rows, lanes, total):
        mixed[rows, lanes] = total

    convolve(pad, shifted, taps, height, breadth, False, store)
    mean = jnp.sum(mixed[...], axis=1, keepdims=True) * (1.0 / channels)
    first = mean.astype(BF16).astype(F32)
    second = (mean - first).astype(BF16).astype(F32)
    message[:cells, :] = ((mixed[...] - first) - second).astype(BF16)
    tail[...] = jnp.zeros_like(tail)
    per = cells // channels
    for t, column in enumerate((first, second)):
        flat = jnp.broadcast_to(column, (cells, 128)).T
        for p in range(per):
            tail[t * per + p : t * per + p + 1, :] = flat[:1, p * channels : (p + 1) * channels]
    for t, part in enumerate(split3(gain[...])):
        tail[2 * per + t : 2 * per + t + 1, :] = part.astype(F32)
    message[cells : message.shape[0] - cells, :] = tail[...].astype(BF16)
    message[message.shape[0] - cells :, :] = upstream[...]


def copy_pieces(pieces, refs, whole, sems):
    copies = []
    for n, (ref, (row_at, column_at)) in enumerate(zip(refs, pieces)):
        rows, columns = ref.shape
        row, column = row_at(), column_at()
        copy = pltpu.make_async_copy(
            ref,
            whole.at[
                pl.ds(row if isinstance(row, int) else pl.multiple_of(row, rows), rows),
                pl.ds(column if isinstance(column, int) else pl.multiple_of(column, columns), columns),
            ],
            sems.at[n],
        )
        copy.start()
        copies.append(copy)
    return copies


def mlp_kernel(in_pieces, out_pieces, n_col, *refs):
    messages, refs = refs[:n_col], refs[n_col:]
    in_refs, refs = refs[: len(in_pieces)], refs[len(in_pieces) :]
    out_refs, refs = refs[: len(out_pieces)], refs[len(out_pieces) :]
    outs, refs = refs[:n_col], refs[n_col:]
    hidden, whole, whole_out, normed, scaled, act_grad, in_sems, out_sems = refs
    copies = copy_pieces(in_pieces, in_refs, whole, in_sems)
    out_copies = copy_pieces(out_pieces, out_refs, whole_out, out_sems)
    cells, channels = outs[0].shape
    up_at = messages[0].shape[0] - cells
    all_channels = n_col * channels
    per = cells // channels

    means, gains = [], []
    for message in messages:
        tail = message[cells:up_at, :].astype(F32)
        flat = tail[:per, :] + tail[per : 2 * per, :]
        row = jnp.concatenate([flat[p : p + 1, :] for p in range(per)], axis=1)
        means.append(jnp.broadcast_to(row, (128, cells)).T[:, :1])
        gains.append(tail[2 * per : 2 * per + 1, :] + tail[2 * per + 1 : 2 * per + 2, :] + tail[2 * per + 2 : 2 * per + 3, :])
    centre = sum(means) * (1.0 / n_col)
    spread = jnp.zeros((cells, 1), F32)
    for k, message in enumerate(messages):
        centred = message[:cells, :].astype(F32) + (means[k] - centre)
        normed[k] = centred
        spread += jnp.sum(centred * centred, axis=1, keepdims=True)
    inv_std = lax.rsqrt(spread * (1.0 / all_channels) + EPSILON)
    for k in range(n_col):
        value = normed[k] * inv_std
        normed[k] = value
        scaled[:, k * channels : (k + 1) * channels] = (value * gains[k]).astype(BF16)
    for copy in copies:
        copy.wait()
    for copy in out_copies:
        copy.wait()
    width = hidden.shape[1]
    tile = min(256, width)
    for start in range(0, width, tile):
        hidden_grad = jnp.zeros((cells, tile), F32)
        for k, message in enumerate(messages):
            hidden_grad += lax.dot_general(
                message[up_at:, :],
                whole_out[start : start + tile, k * channels : (k + 1) * channels],
                (((1,), (1,)), ((), ())),
                preferred_element_type=F32,
            )
        preact = jnp.dot(scaled[...], whole[:, start : start + tile], preferred_element_type=F32)
        phi = 0.5 * (1.0 + lax.erf(preact * math.sqrt(0.5)))
        hidden[:, start : start + tile] = (preact * phi).astype(BF16)
        slope = phi + preact * jnp.exp(-0.5 * preact * preact) * (1.0 / math.sqrt(2.0 * math.pi))
        act_grad[:, start : start + tile] = (hidden_grad * slope).astype(BF16)
    first, second = jnp.zeros((cells, 1), F32), jnp.zeros((cells, 1), F32)
    grads = []
    for k in range(n_col):
        grad = lax.dot_general(
            act_grad[...],
            whole[k * channels : (k + 1) * channels, :],
            (((1,), (1,)), ((), ())),
            preferred_element_type=F32,
        ) * gains[k]
        grads.append(grad)
        first += jnp.sum(grad, axis=1, keepdims=True)
        second += jnp.sum(grad * normed[k], axis=1, keepdims=True)
    first, second = first * (1.0 / all_channels), second * (1.0 / all_channels)
    for k in range(n_col):
        outs[k][...] = (inv_std * (grads[k] - first - normed[k] * second)).astype(BF16)


def branch_kernel(pieces, n_col, hidden, *refs):
    weights, refs = refs[: len(pieces)], refs[len(pieces) :]
    outs, (whole, sems) = refs[:n_col], refs[n_col:]
    copies = copy_pieces(pieces, weights, whole, sems)
    channels = outs[0].shape[1]
    for copy in copies:
        copy.wait()
    for k in range(n_col):
        outs[k][...] = jnp.dot(
            hidden[...], whole[:, k * channels : (k + 1) * channels], preferred_element_type=F32
        ).astype(BF16)


def grad_sum_kernel(dims, n_col, *refs):
    parts, (total, *outs, blocks) = refs[:n_col], refs[n_col:]
    for lane in range(blocks.shape[0]):
        lanes = slice(lane * 128, (lane + 1) * 128)
        blocks[lane] = sum(part[:, lanes].astype(F32) for part in parts)
        total[:, lanes] = blocks[lane]
    emit_top(blocks, outs, *dims)


def backward_conv_kernel(dims, n_top, n_side, grad, taps, upstream, *refs):
    tops, columns, refs = refs[:n_top], refs[n_top : n_top + n_side], refs[n_top + n_side :]
    out, pad, shifted = refs
    height, breadth = dims
    fill_padded(pad, grad, tops, columns, height, breadth)

    def store(rows, lanes, total):
        out[rows, lanes] = total + upstream[rows, lanes].astype(F32)

    convolve(pad, shifted, taps, height, breadth, True, store)


def call(name, vmem, kernel, out_shape, in_specs, scratch, flops=0, bytes_accessed=1 << 20, transcendentals=0):
    return pl.pallas_call(
        kernel,
        name=name,
        out_shape=out_shape,
        in_specs=in_specs,
        out_specs=jax.tree.map(lambda _: pl.BlockSpec(memory_space=pltpu.VMEM), out_shape),
        scratch_shapes=scratch,
        compiler_params=pltpu.CompilerParams(vmem_limit_bytes=vmem),
        cost_estimate=pl.CostEstimate(
            flops=flops, bytes_accessed=bytes_accessed, transcendentals=transcendentals
        ),
    )


IN_VMEM = pl.BlockSpec(memory_space=pltpu.VMEM)
ANYWHERE = pl.BlockSpec(memory_space=pl.ANY)


def tie(x, *others):
    return lax.optimization_barrier((x, others))[0]


def exchangeable():
    n_sec, n_row, n_col = (lax.axis_size(a) for a in ("section", "row", "col"))
    return n_row == n_col and not n_row & (n_row - 1) and not n_sec & (n_sec - 1)


def weights_begin(w_in, w_out):
    n_sec, n_row, n_col = (lax.axis_size(a) for a in ("section", "row", "col"))
    if not exchangeable():
        return None, None, []
    share = w_in.shape[1] // n_sec
    mine_out = lax.dynamic_slice_in_dim(w_out, lax.axis_index("section") * share, share, 0)
    with jax.named_scope("w_out_transposed"):
        mine_out = lax.ppermute(
            mine_out,
            ("row", "col"),
            [(r * n_col + z, z * n_col + r) for r in range(n_row) for z in range(n_col)],
        )
    early = {(0, None): w_in}
    for bit in bits_of(n_row)[1:]:
        early |= {(r ^ bit, None): swap(x, "row", bit, "w_in_row") for (r, _), x in early.items()}
    return mine_out, early, [swap(w_in, "row", bit, "w_in_core") for bit in bits_of(n_row)[:1]]


def weights_finish(w_in, w_out, mine_out, got_in, core_in, message, messages):
    n_sec, n_row, n_col = (lax.axis_size(a) for a in ("section", "row", "col"))
    channels, hidden = w_in.shape[0] * n_row // n_col, w_in.shape[1]
    if not exchangeable():
        order = jnp.arange(n_col) ^ lax.axis_index("col")
        whole_in = lax.all_gather(w_in, "row", axis=0, tiled=True)
        whole_in = whole_in.reshape(n_col, channels, hidden)[order].reshape(-1, hidden)
        whole_out = lax.all_gather(w_out, "row", axis=0, tiled=True)
        whole_out = lax.all_to_all(whole_out, "col", 0, 1, tiled=True)
        whole_out = whole_out.reshape(hidden, n_col, channels)[:, order].reshape(hidden, -1)
        none = (lambda: 0, lambda: 0)
        return [whole_in], [none], [whole_out], [none]

    share = hidden // n_sec

    def place(row_bits, sec_bits):
        block = lambda: ((lax.axis_index("row") ^ row_bits) ^ lax.axis_index("col")) * channels
        part = (lambda: 0) if sec_bits is None else (lambda: (lax.axis_index("section") ^ sec_bits) * share)
        return block, part

    far, core = [b for b in bits_of(n_row) if b > 1], bits_of(n_row)[:1]
    got_out = {(0, 0): tie(mine_out, message, list(got_in.values()))}
    for bit in far:
        got_out |= {(r ^ bit, s): swap(x, "row", bit, "w_out_row") for (r, s), x in got_out.items()}
    for bit in bits_of(n_sec):
        got_out |= {
            (r, s ^ bit): swap(x, "section", bit, f"w_out_section_{r}") for (r, s), x in got_out.items()
        }
    for bit in core:
        got_in |= {
            (r ^ bit, s): core_in[0] if r == 0 else swap(tie(x, messages), "row", bit, f"w_in_core_{r}")
            for (r, s), x in got_in.items()
        }
        first = {
            (r ^ bit, s): swap(tie(x, messages), "row", bit, f"w_out_core_{r}_{s}")
            for (r, s), x in got_out.items()
            if not (r and s)
        }
        got_out |= first | {
            (r ^ bit, s): swap(tie(x, list(first.values())), "row", bit, f"w_out_core_{r}_{s}")
            for (r, s), x in got_out.items()
            if r and s
        }
    return (
        list(got_in.values()),
        [place(*k) for k in got_in],
        list(got_out.values()),
        [place(*k)[::-1] for k in got_out],
    )


def local(image, conv_kernel, norm_gain, w_in, w_out, upstream):
    height, breadth, channels = image.shape
    dims = (height, breadth)
    cells = height * breadth
    n_sec, n_row, n_col = (lax.axis_size(a) for a in ("section", "row", "col"))
    all_channels, hidden = n_col * channels, w_in.shape[1]
    top = jax.ShapeDtypeStruct((MARGIN * breadth, channels), BF16)
    side = jax.ShapeDtypeStruct((side_rows(height), channels), BF16)
    n_top, n_side = len(pairings(n_sec)), len(pairings(n_row))
    padded = [
        pltpu.VMEM((channels // 128, (height + 2 * MARGIN) * padded_width(breadth), 128), F32),
        pltpu.VMEM((KERNEL, (height + 2 * MARGIN) * breadth, 128), F32),
    ]
    conv_cost = dict(flops=2 * KERNEL * KERNEL * cells * channels * 30)

    def columns_of(cell_values, tops, name):
        sent = call(
            name,
            4 * MIB,
            functools.partial(sides_kernel, dims, n_top),
            [side] * n_side,
            [IN_VMEM] * (1 + n_top),
            [pltpu.VMEM((channels // 128, (height + 2 * MARGIN) * breadth, 128), F32)],
        )(cell_values, *tops)
        return meet(sent, "row", name)

    def to_col(parts, name):
        with jax.named_scope(name):
            return [p if k == 0 else swap(p, "col", k) for k, p in enumerate(parts)]

    flat_image = image.reshape(cells, channels)
    flat_up = upstream.reshape(cells, channels)
    mine_out, early_in, core_in = weights_begin(w_in, w_out)
    size = MARGIN * breadth
    sent = [
        lax.dynamic_slice_in_dim(
            flat_image, jnp.where(faces_up(lax.axis_index("section"), p), cells - size, 0), size, 0
        )
        for p in range(n_top)
    ]
    tops = meet(sent, "section", "image_rows")
    columns = columns_of(flat_image, tops, "image_columns")
    rows = message_rows(cells, channels)
    message = call(
        "forward_conv",
        8 * MIB,
        functools.partial(forward_conv_kernel, dims, n_top, n_side),
        jax.ShapeDtypeStruct((rows, channels), BF16),
        [IN_VMEM] * (4 + n_top + n_side),
        padded + [pltpu.VMEM((cells, channels), F32), pltpu.VMEM((rows - 2 * cells, channels), F32)],
        **conv_cost,
    )(tie(flat_image, core_in), conv_kernel, norm_gain.reshape(1, channels), flat_up, *tops, *columns)

    messages = to_col([message] * n_col, "features")
    in_refs, in_pieces, out_refs, out_pieces = weights_finish(
        w_in, w_out, mine_out, early_in, core_in, message, messages
    )

    product = 2 * cells * all_channels * hidden
    weight = pltpu.VMEM((all_channels, hidden), BF16)
    weight_t = pltpu.VMEM((hidden, all_channels), BF16)
    part = jax.ShapeDtypeStruct((cells, channels), BF16)
    *grads, act = call(
        "mlp",
        20 * MIB,
        functools.partial(mlp_kernel, in_pieces, out_pieces, n_col),
        [part] * n_col + [jax.ShapeDtypeStruct((cells, hidden), BF16)],
        [IN_VMEM] * n_col + [ANYWHERE] * (len(in_refs) + len(out_refs)),
        [
            weight,
            weight_t,
            pltpu.VMEM((n_col, cells, channels), F32),
            pltpu.VMEM((cells, all_channels), BF16),
            pltpu.VMEM((cells, hidden), BF16),
            pltpu.SemaphoreType.DMA((len(in_refs),)),
            pltpu.SemaphoreType.DMA((len(out_refs),)),
        ],
        flops=3 * product,
        transcendentals=2 * cells * hidden,
    )(*messages, *in_refs, *out_refs)
    grads = to_col(grads, "grad_sums")
    act = tie(act, grads[1:3])
    branches = call(
        "branch",
        8 * MIB,
        functools.partial(branch_kernel, out_pieces, n_col),
        [part] * n_col,
        [IN_VMEM] + [ANYWHERE] * len(out_refs),
        [weight_t, pltpu.SemaphoreType.DMA((len(out_refs),))],
        flops=product,
    )(act, *out_refs)
    branches = to_col(branches, "branch_sums")
    mixed_grad, *sent = call(
        "grad_sum",
        4 * MIB,
        functools.partial(grad_sum_kernel, dims, n_col),
        [jax.ShapeDtypeStruct((cells, channels), F32)] + [top] * n_top,
        [IN_VMEM] * n_col,
        [pltpu.VMEM((channels // 128, cells, 128), F32)],
    )(*grads)
    tops = meet(sent, "section", "grad_rows")
    columns = columns_of(mixed_grad, tops, "grad_columns")
    image_grad = call(
        "backward_conv",
        8 * MIB,
        functools.partial(backward_conv_kernel, dims, n_top, n_side),
        jax.ShapeDtypeStruct((cells, channels), F32),
        [IN_VMEM] * (3 + n_top + n_side),
        padded,
        **conv_cost,
    )(mixed_grad, conv_kernel, flat_up, *tops, *columns)
    branches = tie(branches, image_grad)
    output = (flat_image.astype(F32) + sum(b.astype(F32) for b in branches)).astype(BF16)
    return output.reshape(image.shape), image_grad.reshape(image.shape)


def solution(mesh):
    in_specs = (
        P("section", "row", "col"),
        P(None, None, "col"),
        P("col"),
        P("row", "col"),
        P("row", "col"),
        P("section", "row", "col"),
    )
    out_specs = (P("section", "row", "col"), P("section", "row", "col"))
    return jax.shard_map(local, mesh=mesh, in_specs=in_specs, out_specs=out_specs, check_vma=False)
```

```python
import functools
import math

import jax
import jax.numpy as jnp
from jax import lax
from jax.experimental import pallas as pl
from jax.experimental.pallas import tpu as pltpu
from jax.sharding import PartitionSpec as P

KERNEL = 7
MARGIN = KERNEL // 2
EPSILON = 1e-06
BF16, F32 = jnp.bfloat16, jnp.float32
MIB = 1024 * 1024


def round_up(value, to):
    return -(-value // to) * to


def bits_of(count):
    return [1 << b for b in range(count.bit_length() - 1)]


def swap(x, axis, bit, name=None):
    count = lax.axis_size(axis)
    with jax.named_scope(name or f"{axis}_{bit}"):
        return lax.ppermute(x, axis, [(i, i ^ bit) for i in range(count)])


def pairings(count):
    both = [[(i, i + 1) for i in range(first, count - 1, 2)] for first in range(2)]
    return [p + [(b, a) for a, b in p] for p in both if p]


def faces_up(index, pairing):
    return (index + pairing) % 2 == 0


def meet(strips, axis, name):
    with jax.named_scope(name):
        return [
            lax.ppermute(strip, axis, pairs)
            for strip, pairs in zip(strips, pairings(lax.axis_size(axis)))
        ]


def low_high(index, received):
    if not received:
        return None, None
    first = received[0]
    second = received[1] if len(received) > 1 else jnp.zeros_like(first)
    odd = index % 2 == 1
    return jnp.where(odd, first, second), jnp.where(odd, second, first)


def side_rows(height):
    return round_up(MARGIN * (height + 2 * MARGIN), 16)


def emit_top(cells, outs, height, breadth):
    size = MARGIN * breadth
    for pairing, out in enumerate(outs):
        up = faces_up(lax.axis_index("section"), pairing)
        for lane in range(cells.shape[0]):
            out[:, lane * 128 : (lane + 1) * 128] = jnp.where(
                up, cells[lane, height * breadth - size :, :], cells[lane, :size, :]
            ).astype(BF16)


def sides_kernel(dims, n_top, cells, *refs):
    height, breadth = dims
    tops, (*outs, blocks) = refs[:n_top], refs[n_top:]
    size = MARGIN * breadth
    tall = height + 2 * MARGIN
    for lane in range(blocks.shape[0]):
        lanes = slice(lane * 128, (lane + 1) * 128)
        block = blocks.at[lane]
        low, high = low_high(lax.axis_index("section"), [top[:, lanes].astype(F32) for top in tops])
        block[:size, :] = jnp.zeros((size, 128), F32) if low is None else low
        block[size : size + height * breadth, :] = cells[:, lanes].astype(F32)
        block[size + height * breadth :, :] = jnp.zeros((size, 128), F32) if high is None else high
        for pairing, out in enumerate(outs):
            up = faces_up(lax.axis_index("row"), pairing)
            columns = [
                jnp.where(
                    up,
                    block[pl.ds(breadth - MARGIN + j, tall, stride=breadth), :],
                    block[pl.ds(j, tall, stride=breadth), :],
                )
                for j in range(MARGIN)
            ]
            spare = out.shape[0] - MARGIN * tall
            if spare:
                columns.append(jnp.zeros((spare, 128), F32))
            out[:, lanes] = jnp.concatenate(columns, axis=0).astype(BF16)


LEFT = 8


def padded_width(breadth):
    return round_up(LEFT + breadth + MARGIN, 8)


def fill_padded(pad, cells, tops, columns, height, breadth):
    width = padded_width(breadth)
    tall = height + 2 * MARGIN
    for lane in range(pad.shape[0]):
        block, lanes = pad.at[lane], slice(lane * 128, (lane + 1) * 128)
        for i in range(height):
            start = (MARGIN + i) * width + LEFT
            block[start : start + breadth, :] = cells[i * breadth : (i + 1) * breadth, lanes].astype(F32)
        low, high = low_high(lax.axis_index("section"), [top[:, lanes].astype(F32) for top in tops])
        for i in range(MARGIN):
            for row, strip in ((i, low), (MARGIN + height + i, high)):
                start = row * width + LEFT
                block[start : start + breadth, :] = (
                    jnp.zeros((breadth, 128), F32)
                    if strip is None
                    else strip[i * breadth : (i + 1) * breadth, :]
                )
        low, high = low_high(lax.axis_index("row"), [c[:, lanes].astype(F32) for c in columns])
        for j in range(MARGIN):
            for column, strip in ((LEFT - MARGIN + j, low), (LEFT + breadth + j, high)):
                block[pl.ds(column, tall, stride=width), :] = (
                    jnp.zeros((tall, 128), F32)
                    if strip is None
                    else strip[j * tall : (j + 1) * tall, :]
                )


def convolve(pad, shifted, taps, height, breadth, flip, store):
    width = padded_width(breadth)
    tall = height + 2 * MARGIN
    step = 4 if height % 4 == 0 else 1
    for lane in range(pad.shape[0]):
        lanes = slice(lane * 128, (lane + 1) * 128)
        for b in range(KERNEL):
            for i in range(tall):
                start = i * width + LEFT - MARGIN + b
                shifted[b, i * breadth : (i + 1) * breadth, :] = pad[lane, start : start + breadth, :]
        for top in range(0, height, step):
            total = jnp.zeros((step * breadth, 128), F32)
            for a in range(KERNEL):
                for b in range(KERNEL):
                    p, q = (KERNEL - 1 - a, KERNEL - 1 - b) if flip else (a, b)
                    first = (top + a) * breadth
                    total += shifted[b, first : first + step * breadth, :] * taps[p, q, lanes][None, :]
            store(slice(top * breadth, (top + step) * breadth), lanes, total)


def split3(x):
    high = x.astype(BF16)
    left = x - high.astype(F32)
    mid = left.astype(BF16)
    return high, mid, (left - mid.astype(F32)).astype(BF16)


def message_rows(cells, channels):
    return 2 * cells + round_up(2 * (cells // channels) + 3, 16)


def forward_conv_kernel(dims, n_top, n_side, image, taps, gain, upstream, *refs):
    tops, columns, refs = refs[:n_top], refs[n_top : n_top + n_side], refs[n_top + n_side :]
    message, pad, shifted, mixed, tail = refs
    height, breadth = dims
    cells, channels = image.shape
    fill_padded(pad, image, tops, columns, height, breadth)

    def store(rows, lanes, total):
        mixed[rows, lanes] = total

    convolve(pad, shifted, taps, height, breadth, False, store)
    mean = jnp.sum(mixed[...], axis=1, keepdims=True) * (1.0 / channels)
    first = mean.astype(BF16).astype(F32)
    second = (mean - first).astype(BF16).astype(F32)
    message[:cells, :] = ((mixed[...] - first) - second).astype(BF16)
    tail[...] = jnp.zeros_like(tail)
    per = cells // channels
    for t, column in enumerate((first, second)):
        flat = jnp.broadcast_to(column, (cells, 128)).T
        for p in range(per):
            tail[t * per + p : t * per + p + 1, :] = flat[:1, p * channels : (p + 1) * channels]
    for t, part in enumerate(split3(gain[...])):
        tail[2 * per + t : 2 * per + t + 1, :] = part.astype(F32)
    message[cells : message.shape[0] - cells, :] = tail[...].astype(BF16)
    message[message.shape[0] - cells :, :] = upstream[...]


def copy_pieces(pieces, refs, whole, sems):
    copies = []
    for n, (ref, (row_at, column_at)) in enumerate(zip(refs, pieces)):
        rows, columns = ref.shape
        row, column = row_at(), column_at()
        copy = pltpu.make_async_copy(
            ref,
            whole.at[
                pl.ds(row if isinstance(row, int) else pl.multiple_of(row, rows), rows),
                pl.ds(column if isinstance(column, int) else pl.multiple_of(column, columns), columns),
            ],
            sems.at[n],
        )
        copy.start()
        copies.append(copy)
    return copies


def mlp_kernel(in_pieces, out_pieces, n_col, *refs):
    messages, refs = refs[:n_col], refs[n_col:]
    in_refs, refs = refs[: len(in_pieces)], refs[len(in_pieces) :]
    out_refs, refs = refs[: len(out_pieces)], refs[len(out_pieces) :]
    outs, refs = refs[:n_col], refs[n_col:]
    hidden, whole, whole_out, normed, scaled, act_grad, in_sems, out_sems = refs
    copies = copy_pieces(in_pieces, in_refs, whole, in_sems)
    out_copies = copy_pieces(out_pieces, out_refs, whole_out, out_sems)
    cells, channels = outs[0].shape
    up_at = messages[0].shape[0] - cells
    all_channels = n_col * channels
    per = cells // channels

    means, gains = [], []
    for message in messages:
        tail = message[cells:up_at, :].astype(F32)
        flat = tail[:per, :] + tail[per : 2 * per, :]
        row = jnp.concatenate([flat[p : p + 1, :] for p in range(per)], axis=1)
        means.append(jnp.broadcast_to(row, (128, cells)).T[:, :1])
        gains.append(tail[2 * per : 2 * per + 1, :] + tail[2 * per + 1 : 2 * per + 2, :] + tail[2 * per + 2 : 2 * per + 3, :])
    centre = sum(means) * (1.0 / n_col)
    spread = jnp.zeros((cells, 1), F32)
    for k, message in enumerate(messages):
        centred = message[:cells, :].astype(F32) + (means[k] - centre)
        normed[k] = centred
        spread += jnp.sum(centred * centred, axis=1, keepdims=True)
    inv_std = lax.rsqrt(spread * (1.0 / all_channels) + EPSILON)
    for k in range(n_col):
        value = normed[k] * inv_std
        normed[k] = value
        scaled[:, k * channels : (k + 1) * channels] = (value * gains[k]).astype(BF16)
    for copy in copies:
        copy.wait()
    for copy in out_copies:
        copy.wait()
    width = hidden.shape[1]
    tile = min(256, width)
    for start in range(0, width, tile):
        hidden_grad = jnp.zeros((cells, tile), F32)
        for k, message in enumerate(messages):
            hidden_grad += lax.dot_general(
                message[up_at:, :],
                whole_out[start : start + tile, k * channels : (k + 1) * channels],
                (((1,), (1,)), ((), ())),
                preferred_element_type=F32,
            )
        preact = jnp.dot(scaled[...], whole[:, start : start + tile], preferred_element_type=F32)
        phi = 0.5 * (1.0 + lax.erf(preact * math.sqrt(0.5)))
        hidden[:, start : start + tile] = (preact * phi).astype(BF16)
        slope = phi + preact * jnp.exp(-0.5 * preact * preact) * (1.0 / math.sqrt(2.0 * math.pi))
        act_grad[:, start : start + tile] = (hidden_grad * slope).astype(BF16)
    first, second = jnp.zeros((cells, 1), F32), jnp.zeros((cells, 1), F32)
    grads = []
    for k in range(n_col):
        grad = lax.dot_general(
            act_grad[...],
            whole[k * channels : (k + 1) * channels, :],
            (((1,), (1,)), ((), ())),
            preferred_element_type=F32,
        ) * gains[k]
        grads.append(grad)
        first += jnp.sum(grad, axis=1, keepdims=True)
        second += jnp.sum(grad * normed[k], axis=1, keepdims=True)
    first, second = first * (1.0 / all_channels), second * (1.0 / all_channels)
    for k in range(n_col):
        outs[k][...] = (inv_std * (grads[k] - first - normed[k] * second)).astype(BF16)


def branch_kernel(pieces, n_col, hidden, *refs):
    weights, refs = refs[: len(pieces)], refs[len(pieces) :]
    outs, (whole, sems) = refs[:n_col], refs[n_col:]
    copies = copy_pieces(pieces, weights, whole, sems)
    channels = outs[0].shape[1]
    for copy in copies:
        copy.wait()
    for k in range(n_col):
        outs[k][...] = jnp.dot(
            hidden[...], whole[:, k * channels : (k + 1) * channels], preferred_element_type=F32
        ).astype(BF16)


def grad_sum_kernel(dims, n_col, *refs):
    parts, (total, *outs, blocks) = refs[:n_col], refs[n_col:]
    for lane in range(blocks.shape[0]):
        lanes = slice(lane * 128, (lane + 1) * 128)
        blocks[lane] = sum(part[:, lanes].astype(F32) for part in parts)
        total[:, lanes] = blocks[lane]
    emit_top(blocks, outs, *dims)


def backward_conv_kernel(dims, n_top, n_side, grad, taps, upstream, *refs):
    tops, columns, refs = refs[:n_top], refs[n_top : n_top + n_side], refs[n_top + n_side :]
    out, pad, shifted = refs
    height, breadth = dims
    fill_padded(pad, grad, tops, columns, height, breadth)

    def store(rows, lanes, total):
        out[rows, lanes] = total + upstream[rows, lanes].astype(F32)

    convolve(pad, shifted, taps, height, breadth, True, store)


def call(name, vmem, kernel, out_shape, in_specs, scratch, flops=0, bytes_accessed=1 << 20, transcendentals=0):
    return pl.pallas_call(
        kernel,
        name=name,
        out_shape=out_shape,
        in_specs=in_specs,
        out_specs=jax.tree.map(lambda _: pl.BlockSpec(memory_space=pltpu.VMEM), out_shape),
        scratch_shapes=scratch,
        compiler_params=pltpu.CompilerParams(vmem_limit_bytes=vmem),
        cost_estimate=pl.CostEstimate(
            flops=flops, bytes_accessed=bytes_accessed, transcendentals=transcendentals
        ),
    )


IN_VMEM = pl.BlockSpec(memory_space=pltpu.VMEM)
ANYWHERE = pl.BlockSpec(memory_space=pl.ANY)


def tie(x, *others):
    return lax.optimization_barrier((x, others))[0]


def exchangeable():
    n_sec, n_row, n_col = (lax.axis_size(a) for a in ("section", "row", "col"))
    return n_row == n_col and not n_row & (n_row - 1) and not n_sec & (n_sec - 1)


def weights_begin(w_in, w_out):
    n_sec, n_row, n_col = (lax.axis_size(a) for a in ("section", "row", "col"))
    if not exchangeable():
        return None, None, []
    share = w_in.shape[1] // n_sec
    mine_out = lax.dynamic_slice_in_dim(w_out, lax.axis_index("section") * share, share, 0)
    with jax.named_scope("w_out_transposed"):
        mine_out = lax.ppermute(
            mine_out,
            ("row", "col"),
            [(r * n_col + z, z * n_col + r) for r in range(n_row) for z in range(n_col)],
        )
    early = {(0, None): w_in}
    for bit in bits_of(n_row)[1:]:
        early |= {(r ^ bit, None): swap(x, "row", bit, "w_in_row") for (r, _), x in early.items()}
    return mine_out, early, [swap(w_in, "row", bit, "w_in_core") for bit in bits_of(n_row)[:1]]


def weights_far(mine_out, others):
    if not exchangeable():
        return None, []
    got = {(0, 0): tie(mine_out, others)}
    for bit in bits_of(lax.axis_size("row"))[1:]:
        got |= {(r ^ bit, s): swap(x, "row", bit, "w_out_row") for (r, s), x in got.items()}
    for bit in bits_of(lax.axis_size("section")):
        got |= {
            (0, s ^ bit): swap(x, "section", bit, "w_out_section") for (r, s), x in got.items() if r == 0
        }
    return got, list(got.values())


def weights_finish(w_in, w_out, got_out, got_in, core_in, messages):
    n_sec, n_row, n_col = (lax.axis_size(a) for a in ("section", "row", "col"))
    channels, hidden = w_in.shape[0] * n_row // n_col, w_in.shape[1]
    if not exchangeable():
        order = jnp.arange(n_col) ^ lax.axis_index("col")
        whole_in = lax.all_gather(w_in, "row", axis=0, tiled=True)
        whole_in = whole_in.reshape(n_col, channels, hidden)[order].reshape(-1, hidden)
        whole_out = lax.all_gather(w_out, "row", axis=0, tiled=True)
        whole_out = lax.all_to_all(whole_out, "col", 0, 1, tiled=True)
        whole_out = whole_out.reshape(hidden, n_col, channels)[:, order].reshape(hidden, -1)
        none = (lambda: 0, lambda: 0)
        return [whole_in], [none], [whole_out], [none]

    share = hidden // n_sec

    def place(row_bits, sec_bits):
        block = lambda: ((lax.axis_index("row") ^ row_bits) ^ lax.axis_index("col")) * channels
        part = (lambda: 0) if sec_bits is None else (lambda: (lax.axis_index("section") ^ sec_bits) * share)
        return block, part

    core = bits_of(n_row)[:1]
    for bit in bits_of(n_sec):
        got_out |= {
            (r, s ^ bit): swap(x, "section", bit, "w_out_both") for (r, s), x in got_out.items() if r and s < bit
        }
    for bit in core:
        got_in |= {
            (r ^ bit, s): core_in[0] if r == 0 else swap(x, "row", bit, f"w_in_core_{r}")
            for (r, s), x in got_in.items()
        }
        gate = swap(tie(got_out[0, 0], messages), "row", bit, "w_out_core_0_0")
        got_out |= {(bit, 0): gate} | {
            (r ^ bit, s): swap(tie(x, gate) if r and s else x, "row", bit, f"w_out_core_{r}_{s}")
            for (r, s), x in got_out.items()
            if r or s
        }
    return (
        list(got_in.values()),
        [place(*k) for k in got_in],
        list(got_out.values()),
        [place(*k)[::-1] for k in got_out],
    )


def local(image, conv_kernel, norm_gain, w_in, w_out, upstream):
    height, breadth, channels = image.shape
    dims = (height, breadth)
    cells = height * breadth
    n_sec, n_row, n_col = (lax.axis_size(a) for a in ("section", "row", "col"))
    all_channels, hidden = n_col * channels, w_in.shape[1]
    top = jax.ShapeDtypeStruct((MARGIN * breadth, channels), BF16)
    side = jax.ShapeDtypeStruct((side_rows(height), channels), BF16)
    n_top, n_side = len(pairings(n_sec)), len(pairings(n_row))
    padded = [
        pltpu.VMEM((channels // 128, (height + 2 * MARGIN) * padded_width(breadth), 128), F32),
        pltpu.VMEM((KERNEL, (height + 2 * MARGIN) * breadth, 128), F32),
    ]
    conv_cost = dict(flops=2 * KERNEL * KERNEL * cells * channels * 30)

    def columns_of(cell_values, tops, name):
        sent = call(
            name,
            4 * MIB,
            functools.partial(sides_kernel, dims, n_top),
            [side] * n_side,
            [IN_VMEM] * (1 + n_top),
            [pltpu.VMEM((channels // 128, (height + 2 * MARGIN) * breadth, 128), F32)],
        )(cell_values, *tops)
        return meet(sent, "row", name)

    def to_col(parts, name):
        with jax.named_scope(name):
            return [p if k == 0 else swap(p, "col", k) for k, p in enumerate(parts)]

    def gather_col(part, name, others):
        got = {0: part}
        with jax.named_scope(name):
            for bit in reversed(bits_of(n_col)):
                got |= {k ^ bit: swap(tie(x, others) if k else x, "col", bit) for k, x in got.items()}
        return [got[k] for k in range(n_col)]

    def scatter_col(parts, name, others):
        terms = [[p] for p in parts]
        with jax.named_scope(name):
            for bit in bits_of(n_col):
                for k in range(bit, n_col, 2 * bit):
                    far, *more = terms[k]
                    if more:
                        more = tie(more, others)
                        far = sum((m.astype(F32) for m in more), far.astype(F32)).astype(BF16)
                    terms[k ^ bit].append(swap(far, "col", bit))
        return terms[0]

    flat_image = image.reshape(cells, channels)
    flat_up = upstream.reshape(cells, channels)
    mine_out, early_in, core_in = weights_begin(w_in, w_out)
    size = MARGIN * breadth
    sent = [
        lax.dynamic_slice_in_dim(
            flat_image, jnp.where(faces_up(lax.axis_index("section"), p), cells - size, 0), size, 0
        )
        for p in range(n_top)
    ]
    tops = meet(sent, "section", "image_rows")
    columns = columns_of(flat_image, tops, "image_columns")
    rows = message_rows(cells, channels)
    message = call(
        "forward_conv",
        8 * MIB,
        functools.partial(forward_conv_kernel, dims, n_top, n_side),
        jax.ShapeDtypeStruct((rows, channels), BF16),
        [IN_VMEM] * (4 + n_top + n_side),
        padded + [pltpu.VMEM((cells, channels), F32), pltpu.VMEM((rows - 2 * cells, channels), F32)],
        **conv_cost,
    )(tie(flat_image, core_in), conv_kernel, norm_gain.reshape(1, channels), flat_up, *tops, *columns)

    early = [] if early_in is None else list(early_in.values())
    got_out, rows_done = weights_far(mine_out, [message, early])
    messages = gather_col(message, "features", rows_done)
    in_refs, in_pieces, out_refs, out_pieces = weights_finish(
        w_in, w_out, got_out, early_in, core_in, messages
    )

    product = 2 * cells * all_channels * hidden
    weight = pltpu.VMEM((all_channels, hidden), BF16)
    weight_t = pltpu.VMEM((hidden, all_channels), BF16)
    part = jax.ShapeDtypeStruct((cells, channels), BF16)
    *grads, act = call(
        "mlp",
        20 * MIB,
        functools.partial(mlp_kernel, in_pieces, out_pieces, n_col),
        [part] * n_col + [jax.ShapeDtypeStruct((cells, hidden), BF16)],
        [IN_VMEM] * n_col + [ANYWHERE] * (len(in_refs) + len(out_refs)),
        [
            weight,
            weight_t,
            pltpu.VMEM((n_col, cells, channels), F32),
            pltpu.VMEM((cells, all_channels), BF16),
            pltpu.VMEM((cells, hidden), BF16),
            pltpu.SemaphoreType.DMA((len(in_refs),)),
            pltpu.SemaphoreType.DMA((len(out_refs),)),
        ],
        flops=3 * product,
        transcendentals=2 * cells * hidden,
    )(*messages, *in_refs, *out_refs)
    grads = to_col(grads, "grad_sums")
    act = tie(act, grads[1])
    branches = call(
        "branch",
        8 * MIB,
        functools.partial(branch_kernel, out_pieces, n_col),
        [part] * n_col,
        [IN_VMEM] + [ANYWHERE] * len(out_refs),
        [weight_t, pltpu.SemaphoreType.DMA((len(out_refs),))],
        flops=product,
    )(act, *out_refs)
    mixed_grad, *sent = call(
        "grad_sum",
        4 * MIB,
        functools.partial(grad_sum_kernel, dims, n_col),
        [jax.ShapeDtypeStruct((cells, channels), F32)] + [top] * n_top,
        [IN_VMEM] * n_col,
        [pltpu.VMEM((channels // 128, cells, 128), F32)],
    )(*grads)
    tops = meet(sent, "section", "grad_rows")
    branches = scatter_col(branches, "branch_sums", tops)
    columns = columns_of(mixed_grad, tops, "grad_columns")
    image_grad = call(
        "backward_conv",
        8 * MIB,
        functools.partial(backward_conv_kernel, dims, n_top, n_side),
        jax.ShapeDtypeStruct((cells, channels), F32),
        [IN_VMEM] * (3 + n_top + n_side),
        padded,
        **conv_cost,
    )(mixed_grad, conv_kernel, flat_up, *tops, *columns)
    branches = tie(branches, image_grad)
    output = (flat_image.astype(F32) + sum(b.astype(F32) for b in branches)).astype(BF16)
    return output.reshape(image.shape), image_grad.reshape(image.shape)


def solution(mesh):
    in_specs = (
        P("section", "row", "col"),
        P(None, None, "col"),
        P("col"),
        P("row", "col"),
        P("row", "col"),
        P("section", "row", "col"),
    )
    out_specs = (P("section", "row", "col"), P("section", "row", "col"))
    return jax.shard_map(local, mesh=mesh, in_specs=in_specs, out_specs=out_specs, check_vma=False)
```

```python
import functools
import math

import jax
import jax.numpy as jnp
from jax import lax
from jax.experimental import pallas as pl
from jax.experimental.pallas import tpu as pltpu
from jax.sharding import PartitionSpec as P

KERNEL = 7
MARGIN = KERNEL // 2
EPSILON = 1e-06
BF16, F32 = jnp.bfloat16, jnp.float32
MIB = 1024 * 1024


def round_up(value, to):
    return -(-value // to) * to


def bits_of(count):
    return [1 << b for b in range(count.bit_length() - 1)]


def swap(x, axis, bit, name=None):
    count = lax.axis_size(axis)
    with jax.named_scope(name or f"{axis}_{bit}"):
        return lax.ppermute(x, axis, [(i, i ^ bit) for i in range(count)])


def pairings(count):
    both = [[(i, i + 1) for i in range(first, count - 1, 2)] for first in range(2)]
    return [p + [(b, a) for a, b in p] for p in both if p]


def faces_up(index, pairing):
    return (index + pairing) % 2 == 0


def meet(strips, axis, name):
    with jax.named_scope(name):
        return [
            lax.ppermute(strip, axis, pairs)
            for strip, pairs in zip(strips, pairings(lax.axis_size(axis)))
        ]


def low_high(index, received):
    if not received:
        return None, None
    first = received[0]
    second = received[1] if len(received) > 1 else jnp.zeros_like(first)
    odd = index % 2 == 1
    return jnp.where(odd, first, second), jnp.where(odd, second, first)


def side_rows(height):
    return round_up(MARGIN * (height + 2 * MARGIN), 16)


def emit_top(cells, outs, height, breadth):
    size = MARGIN * breadth
    for pairing, out in enumerate(outs):
        up = faces_up(lax.axis_index("section"), pairing)
        for lane in range(cells.shape[0]):
            out[:, lane * 128 : (lane + 1) * 128] = jnp.where(
                up, cells[lane, height * breadth - size :, :], cells[lane, :size, :]
            ).astype(BF16)


def sides_kernel(dims, n_top, cells, *refs):
    height, breadth = dims
    tops, (*outs, blocks) = refs[:n_top], refs[n_top:]
    size = MARGIN * breadth
    tall = height + 2 * MARGIN
    for lane in range(blocks.shape[0]):
        lanes = slice(lane * 128, (lane + 1) * 128)
        block = blocks.at[lane]
        low, high = low_high(lax.axis_index("section"), [top[:, lanes].astype(F32) for top in tops])
        block[:size, :] = jnp.zeros((size, 128), F32) if low is None else low
        block[size : size + height * breadth, :] = cells[:, lanes].astype(F32)
        block[size + height * breadth :, :] = jnp.zeros((size, 128), F32) if high is None else high
        for pairing, out in enumerate(outs):
            up = faces_up(lax.axis_index("row"), pairing)
            columns = [
                jnp.where(
                    up,
                    block[pl.ds(breadth - MARGIN + j, tall, stride=breadth), :],
                    block[pl.ds(j, tall, stride=breadth), :],
                )
                for j in range(MARGIN)
            ]
            spare = out.shape[0] - MARGIN * tall
            if spare:
                columns.append(jnp.zeros((spare, 128), F32))
            out[:, lanes] = jnp.concatenate(columns, axis=0).astype(BF16)


LEFT = 8


def padded_width(breadth):
    return round_up(LEFT + breadth + MARGIN, 8)


def fill_padded(pad, cells, tops, columns, height, breadth):
    width = padded_width(breadth)
    tall = height + 2 * MARGIN
    for lane in range(pad.shape[0]):
        block, lanes = pad.at[lane], slice(lane * 128, (lane + 1) * 128)
        for i in range(height):
            start = (MARGIN + i) * width + LEFT
            block[start : start + breadth, :] = cells[i * breadth : (i + 1) * breadth, lanes].astype(F32)
        low, high = low_high(lax.axis_index("section"), [top[:, lanes].astype(F32) for top in tops])
        for i in range(MARGIN):
            for row, strip in ((i, low), (MARGIN + height + i, high)):
                start = row * width + LEFT
                block[start : start + breadth, :] = (
                    jnp.zeros((breadth, 128), F32)
                    if strip is None
                    else strip[i * breadth : (i + 1) * breadth, :]
                )
        low, high = low_high(lax.axis_index("row"), [c[:, lanes].astype(F32) for c in columns])
        for j in range(MARGIN):
            for column, strip in ((LEFT - MARGIN + j, low), (LEFT + breadth + j, high)):
                block[pl.ds(column, tall, stride=width), :] = (
                    jnp.zeros((tall, 128), F32)
                    if strip is None
                    else strip[j * tall : (j + 1) * tall, :]
                )


def convolve(pad, shifted, taps, height, breadth, flip, store):
    width = padded_width(breadth)
    tall = height + 2 * MARGIN
    step = 4 if height % 4 == 0 else 1
    for lane in range(pad.shape[0]):
        lanes = slice(lane * 128, (lane + 1) * 128)
        for b in range(KERNEL):
            for i in range(tall):
                start = i * width + LEFT - MARGIN + b
                shifted[b, i * breadth : (i + 1) * breadth, :] = pad[lane, start : start + breadth, :]
        for top in range(0, height, step):
            total = jnp.zeros((step * breadth, 128), F32)
            for a in range(KERNEL):
                for b in range(KERNEL):
                    p, q = (KERNEL - 1 - a, KERNEL - 1 - b) if flip else (a, b)
                    first = (top + a) * breadth
                    total += shifted[b, first : first + step * breadth, :] * taps[p, q, lanes][None, :]
            store(slice(top * breadth, (top + step) * breadth), lanes, total)


def split3(x):
    high = x.astype(BF16)
    left = x - high.astype(F32)
    mid = left.astype(BF16)
    return high, mid, (left - mid.astype(F32)).astype(BF16)


def message_rows(cells, channels):
    return 2 * cells + round_up(2 * (cells // channels) + 3, 16)


def forward_conv_kernel(dims, n_top, n_side, image, taps, gain, upstream, *refs):
    tops, columns, refs = refs[:n_top], refs[n_top : n_top + n_side], refs[n_top + n_side :]
    message, pad, shifted, mixed, tail = refs
    height, breadth = dims
    cells, channels = image.shape
    fill_padded(pad, image, tops, columns, height, breadth)

    def store(rows, lanes, total):
        mixed[rows, lanes] = total

    convolve(pad, shifted, taps, height, breadth, False, store)
    mean = jnp.sum(mixed[...], axis=1, keepdims=True) * (1.0 / channels)
    first = mean.astype(BF16).astype(F32)
    second = (mean - first).astype(BF16).astype(F32)
    message[:cells, :] = ((mixed[...] - first) - second).astype(BF16)
    tail[...] = jnp.zeros_like(tail)
    per = cells // channels
    for t, column in enumerate((first, second)):
        flat = jnp.broadcast_to(column, (cells, 128)).T
        for p in range(per):
            tail[t * per + p : t * per + p + 1, :] = flat[:1, p * channels : (p + 1) * channels]
    for t, part in enumerate(split3(gain[...])):
        tail[2 * per + t : 2 * per + t + 1, :] = part.astype(F32)
    message[cells : message.shape[0] - cells, :] = tail[...].astype(BF16)
    message[message.shape[0] - cells :, :] = upstream[...]


def mlp_kernel(in_slots, out_slots, n_col, *refs):
    messages, refs = refs[:n_col], refs[n_col:]
    in_refs, refs = refs[: len(in_slots)], refs[len(in_slots) :]
    n_out = len(out_slots) * n_col
    out_refs, refs = refs[:n_out], refs[n_out:]
    outs, refs = refs[:n_col], refs[n_col:]
    hidden, normed, scaled, ups, gains, grads, act_grad = refs
    cells, channels = outs[0].shape
    up_at = messages[0].shape[0] - cells
    all_channels = n_col * channels
    per = cells // channels

    means = []
    for k, message in enumerate(messages):
        tail = message[cells:up_at, :].astype(F32)
        flat = tail[:per, :] + tail[per : 2 * per, :]
        row = jnp.concatenate([flat[p : p + 1, :] for p in range(per)], axis=1)
        means.append(jnp.broadcast_to(row, (128, cells)).T[:, :1])
        gains[k] = jnp.broadcast_to(sum(tail[2 * per + t : 2 * per + t + 1, :] for t in range(3)), gains.shape[1:])
        ups[k] = message[up_at:, :]
    centre = sum(means) * (1.0 / n_col)
    spread = jnp.zeros((cells, 1), F32)
    for k, message in enumerate(messages):
        centred = message[:cells, :].astype(F32) + (means[k] - centre)
        normed[k] = centred
        spread += jnp.sum(centred * centred, axis=1, keepdims=True)
    inv_std = lax.rsqrt(spread * (1.0 / all_channels) + EPSILON)
    for k in range(n_col):
        value = normed[k] * inv_std
        normed[k] = value
        scaled[k] = (value * gains[k][:1, :]).astype(BF16)
    share = act_grad.shape[2]
    tile = min(256, share)
    slots = [slot() for slot in in_slots]
    places = []
    for p, (part, blocks) in enumerate(out_slots):
        blocks = [block() for block in blocks]
        place = part() * share
        places.append(place)
        for start in range(0, share, tile):
            columns = pl.ds(pl.multiple_of(place + start, tile), tile)
            preact = sum(
                jnp.dot(scaled[slot], ref[:, columns], preferred_element_type=F32)
                for slot, ref in zip(slots, in_refs)
            )
            hidden_grad = sum(
                lax.dot_general(
                    ups[block],
                    out_refs[p * n_col + j][start : start + tile, :],
                    (((1,), (1,)), ((), ())),
                    preferred_element_type=F32,
                )
                for j, block in enumerate(blocks)
            )
            phi = 0.5 * (1.0 + lax.erf(preact * math.sqrt(0.5)))
            hidden[p, :, start : start + tile] = (preact * phi).astype(BF16)
            slope = phi + preact * jnp.exp(-0.5 * preact * preact) * (1.0 / math.sqrt(2.0 * math.pi))
            act_grad[p, :, start : start + tile] = (hidden_grad * slope).astype(BF16)
    first, second = jnp.zeros((cells, 1), F32), jnp.zeros((cells, 1), F32)
    for slot, ref in zip(slots, in_refs):
        grad = sum(
            lax.dot_general(
                act_grad[p],
                ref[:, pl.ds(pl.multiple_of(place, share), share)],
                (((1,), (1,)), ((), ())),
                preferred_element_type=F32,
            )
            for p, place in enumerate(places)
        ) * gains[slot][:1, :]
        grads[slot] = grad
        first += jnp.sum(grad, axis=1, keepdims=True)
        second += jnp.sum(grad * normed[slot], axis=1, keepdims=True)
    first, second = first * (1.0 / all_channels), second * (1.0 / all_channels)
    for k in range(n_col):
        outs[k][...] = (inv_std * (grads[k] - first - normed[k] * second)).astype(BF16)


def branch_kernel(out_slots, n_col, hidden, *refs):
    n_out = len(out_slots) * n_col
    out_refs, (*outs, whole) = refs[:n_out], refs[n_out:]
    for j in range(n_col):
        whole[out_slots[0][1][j]()] = sum(
            jnp.dot(hidden[p], out_refs[p * n_col + j][...], preferred_element_type=F32)
            for p in range(len(out_slots))
        ).astype(BF16)
    for k in range(n_col):
        outs[k][...] = whole[k]


def grad_sum_kernel(dims, n_col, *refs):
    parts, (total, *outs, blocks) = refs[:n_col], refs[n_col:]
    for lane in range(blocks.shape[0]):
        lanes = slice(lane * 128, (lane + 1) * 128)
        blocks[lane] = sum(part[:, lanes].astype(F32) for part in parts)
        total[:, lanes] = blocks[lane]
    emit_top(blocks, outs, *dims)


def backward_conv_kernel(dims, n_top, n_side, n_terms, grad, taps, upstream, image, *refs):
    tops, columns, refs = refs[:n_top], refs[n_top : n_top + n_side], refs[n_top + n_side :]
    terms, (out, output, pad, shifted) = refs[:n_terms], refs[n_terms:]
    output[...] = (image[...].astype(F32) + sum(term[...].astype(F32) for term in terms)).astype(BF16)
    height, breadth = dims
    fill_padded(pad, grad, tops, columns, height, breadth)

    def store(rows, lanes, total):
        out[rows, lanes] = total + upstream[rows, lanes].astype(F32)

    convolve(pad, shifted, taps, height, breadth, True, store)


def call(name, vmem, kernel, out_shape, in_specs, scratch, flops=0, bytes_accessed=1 << 20, transcendentals=0):
    return pl.pallas_call(
        kernel,
        name=name,
        out_shape=out_shape,
        in_specs=in_specs,
        out_specs=jax.tree.map(lambda _: pl.BlockSpec(memory_space=pltpu.VMEM), out_shape),
        scratch_shapes=scratch,
        compiler_params=pltpu.CompilerParams(vmem_limit_bytes=vmem),
        cost_estimate=pl.CostEstimate(
            flops=flops, bytes_accessed=bytes_accessed, transcendentals=transcendentals
        ),
    )


IN_VMEM = pl.BlockSpec(memory_space=pltpu.VMEM)


def tie(x, *others):
    return lax.optimization_barrier((x, others))[0]


def exchangeable():
    n_sec, n_row, n_col = (lax.axis_size(a) for a in ("section", "row", "col"))
    return n_row == n_col and not n_row & (n_row - 1) and not n_sec & (n_sec - 1)


def weights_begin(w_in, w_out):
    n_sec, n_row, n_col = (lax.axis_size(a) for a in ("section", "row", "col"))
    if not exchangeable():
        return None, None, []
    share = w_in.shape[1] // n_sec
    mine_out = lax.dynamic_slice_in_dim(w_out, lax.axis_index("section") * share, share, 0)
    with jax.named_scope("w_out_transposed"):
        mine_out = lax.ppermute(
            mine_out,
            ("row", "col"),
            [(r * n_col + z, z * n_col + r) for r in range(n_row) for z in range(n_col)],
        )
    early = {(0, None): w_in}
    for bit in bits_of(n_row)[1:]:
        early |= {(r ^ bit, None): swap(x, "row", bit, "w_in_row") for (r, _), x in early.items()}
    return mine_out, early, [swap(w_in, "row", bit, "w_in_core") for bit in bits_of(n_row)[:1]]


def weights_far(mine_out, others):
    if not exchangeable():
        return None, []
    got = {(0, 0): tie(mine_out, others)}
    for bit in bits_of(lax.axis_size("row"))[1:]:
        got |= {(r ^ bit, s): swap(x, "row", bit, "w_out_row") for (r, s), x in got.items()}
    for bit in bits_of(lax.axis_size("section")):
        got |= {
            (0, s ^ bit): swap(x, "section", bit, "w_out_section") for (r, s), x in got.items() if r == 0
        }
    return got, list(got.values())


def weights_finish(w_in, w_out, got_out, got_in, core_in, messages):
    n_sec, n_row, n_col = (lax.axis_size(a) for a in ("section", "row", "col"))
    channels, hidden = w_in.shape[0] * n_row // n_col, w_in.shape[1]
    if not exchangeable():
        order = jnp.arange(n_col) ^ lax.axis_index("col")
        whole_in = lax.all_gather(w_in, "row", axis=0, tiled=True)
        whole_in = whole_in.reshape(n_col, channels, hidden)[order].reshape(-1, hidden)
        whole_out = lax.all_gather(w_out, "row", axis=0, tiled=True)
        whole_out = lax.all_to_all(whole_out, "col", 0, 1, tiled=True)
        whole_out = whole_out.reshape(hidden, n_col, channels)[:, order].reshape(hidden, -1)
        fixed = [functools.partial(int, k) for k in range(n_col)]
        cut = [slice(k * channels, (k + 1) * channels) for k in range(n_col)]
        return [whole_in[c] for c in cut], fixed, [whole_out[:, c] for c in cut], [(functools.partial(int, 0), fixed)]

    def block(row_bits):
        return lambda: (lax.axis_index("row") ^ row_bits) ^ lax.axis_index("col")

    def part(sec_bits):
        return lambda: lax.axis_index("section") ^ sec_bits

    core = bits_of(n_row)[:1]
    for bit in bits_of(n_sec):
        got_out |= {
            (r, s ^ bit): swap(x, "section", bit, "w_out_both") for (r, s), x in got_out.items() if r and s < bit
        }
    for bit in core:
        got_in |= {
            (r ^ bit, s): core_in[0] if r == 0 else swap(x, "row", bit, f"w_in_core_{r}")
            for (r, s), x in got_in.items()
        }
        gate = swap(tie(got_out[0, 0], messages), "row", bit, "w_out_core_0_0")
        got_out |= {(bit, 0): gate} | {
            (r ^ bit, s): swap(tie(x, gate) if r and s else x, "row", bit, f"w_out_core_{r}_{s}")
            for (r, s), x in got_out.items()
            if r or s
        }
    return (
        list(got_in.values()),
        [block(r) for r, _ in got_in],
        [got_out[r, p] for p in range(n_sec) for r in range(n_row)],
        [(part(p), [block(r) for r in range(n_row)]) for p in range(n_sec)],
    )


def local(image, conv_kernel, norm_gain, w_in, w_out, upstream):
    height, breadth, channels = image.shape
    dims = (height, breadth)
    cells = height * breadth
    n_sec, n_row, n_col = (lax.axis_size(a) for a in ("section", "row", "col"))
    all_channels, hidden = n_col * channels, w_in.shape[1]
    top = jax.ShapeDtypeStruct((MARGIN * breadth, channels), BF16)
    side = jax.ShapeDtypeStruct((side_rows(height), channels), BF16)
    n_top, n_side = len(pairings(n_sec)), len(pairings(n_row))
    padded = [
        pltpu.VMEM((channels // 128, (height + 2 * MARGIN) * padded_width(breadth), 128), F32),
        pltpu.VMEM((KERNEL, (height + 2 * MARGIN) * breadth, 128), F32),
    ]
    conv_cost = dict(flops=2 * KERNEL * KERNEL * cells * channels * 30)

    def columns_of(cell_values, tops, name):
        sent = call(
            name,
            4 * MIB,
            functools.partial(sides_kernel, dims, n_top),
            [side] * n_side,
            [IN_VMEM] * (1 + n_top),
            [pltpu.VMEM((channels // 128, (height + 2 * MARGIN) * breadth, 128), F32)],
        )(cell_values, *tops)
        return meet(sent, "row", name)

    def to_col(parts, name):
        with jax.named_scope(name):
            return [p if k == 0 else swap(p, "col", k) for k, p in enumerate(parts)]

    def gather_col(part, name, others):
        got = {0: part}
        with jax.named_scope(name):
            for bit in reversed(bits_of(n_col)):
                got |= {k ^ bit: swap(tie(x, others) if k else x, "col", bit) for k, x in got.items()}
        return [got[k] for k in range(n_col)]

    def scatter_col(parts, name, others):
        terms = [[p] for p in parts]
        with jax.named_scope(name):
            for bit in bits_of(n_col):
                for k in range(bit, n_col, 2 * bit):
                    far, *more = terms[k]
                    if more:
                        more = tie(more, others)
                        far = sum((m.astype(F32) for m in more), far.astype(F32)).astype(BF16)
                    terms[k ^ bit].append(swap(far, "col", bit))
        return terms[0]

    flat_image = image.reshape(cells, channels)
    flat_up = upstream.reshape(cells, channels)
    mine_out, early_in, core_in = weights_begin(w_in, w_out)
    size = MARGIN * breadth
    sent = [
        lax.dynamic_slice_in_dim(
            flat_image, jnp.where(faces_up(lax.axis_index("section"), p), cells - size, 0), size, 0
        )
        for p in range(n_top)
    ]
    tops = meet(sent, "section", "image_rows")
    columns = columns_of(flat_image, tops, "image_columns")
    rows = message_rows(cells, channels)
    message = call(
        "forward_conv",
        8 * MIB,
        functools.partial(forward_conv_kernel, dims, n_top, n_side),
        jax.ShapeDtypeStruct((rows, channels), BF16),
        [IN_VMEM] * (4 + n_top + n_side),
        padded + [pltpu.VMEM((cells, channels), F32), pltpu.VMEM((rows - 2 * cells, channels), F32)],
        **conv_cost,
    )(tie(flat_image, core_in), conv_kernel, norm_gain.reshape(1, channels), flat_up, *tops, *columns)

    early = [] if early_in is None else list(early_in.values())
    got_out, rows_done = weights_far(mine_out, [message, early])
    messages = gather_col(message, "features", rows_done)
    in_refs, in_pieces, out_refs, out_pieces = weights_finish(
        w_in, w_out, got_out, early_in, core_in, messages
    )

    product = 2 * cells * all_channels * hidden
    part = jax.ShapeDtypeStruct((cells, channels), BF16)
    act_shape = (len(out_pieces), cells, hidden // len(out_pieces))
    *grads, act = call(
        "mlp",
        24 * MIB,
        functools.partial(mlp_kernel, in_pieces, out_pieces, n_col),
        [part] * n_col + [jax.ShapeDtypeStruct(act_shape, BF16)],
        [IN_VMEM] * (n_col + len(in_refs) + len(out_refs)),
        [
            pltpu.VMEM((n_col, cells, channels), F32),
            pltpu.VMEM((n_col, cells, channels), BF16),
            pltpu.VMEM((n_col, cells, channels), BF16),
            pltpu.VMEM((n_col, 8, channels), F32),
            pltpu.VMEM((n_col, cells, channels), F32),
            pltpu.VMEM(act_shape, BF16),
        ],
        flops=3 * product,
        transcendentals=2 * cells * hidden,
    )(*messages, *in_refs, *out_refs)
    grads = to_col(grads, "grad_sums")
    act = tie(act, grads[1])
    branches = call(
        "branch",
        12 * MIB,
        functools.partial(branch_kernel, out_pieces, n_col),
        [part] * n_col,
        [IN_VMEM] * (1 + len(out_refs)),
        [pltpu.VMEM((n_col, cells, channels), BF16)],
        flops=product,
    )(act, *out_refs)
    mixed_grad, *sent = call(
        "grad_sum",
        4 * MIB,
        functools.partial(grad_sum_kernel, dims, n_col),
        [jax.ShapeDtypeStruct((cells, channels), F32)] + [top] * n_top,
        [IN_VMEM] * n_col,
        [pltpu.VMEM((channels // 128, cells, 128), F32)],
    )(*grads)
    tops = meet(sent, "section", "grad_rows")
    branches = scatter_col(branches, "branch_sums", tops)
    columns = columns_of(mixed_grad, tops, "grad_columns")
    image_grad, output = call(
        "backward_conv",
        8 * MIB,
        functools.partial(backward_conv_kernel, dims, n_top, n_side, len(branches)),
        [jax.ShapeDtypeStruct((cells, channels), F32), part],
        [IN_VMEM] * (4 + n_top + n_side + len(branches)),
        padded,
        **conv_cost,
    )(mixed_grad, conv_kernel, flat_up, flat_image, *tops, *columns, *branches)
    return output.reshape(image.shape), image_grad.reshape(image.shape)


def solution(mesh):
    in_specs = (
        P("section", "row", "col"),
        P(None, None, "col"),
        P("col"),
        P("row", "col"),
        P("row", "col"),
        P("section", "row", "col"),
    )
    out_specs = (P("section", "row", "col"), P("section", "row", "col"))
    return jax.shard_map(local, mesh=mesh, in_specs=in_specs, out_specs=out_specs, check_vma=False)
```

```python
import functools
import math

import jax
import jax.numpy as jnp
from jax import lax
from jax.experimental import pallas as pl
from jax.experimental.pallas import tpu as pltpu
from jax.sharding import PartitionSpec as P

KERNEL = 7
MARGIN = KERNEL // 2
EPSILON = 1e-06
BF16, F32 = jnp.bfloat16, jnp.float32
MIB = 1024 * 1024


def round_up(value, to):
    return -(-value // to) * to


def bits_of(count):
    return [1 << b for b in range(count.bit_length() - 1)]


def swap(x, axis, bit, name=None):
    count = lax.axis_size(axis)
    with jax.named_scope(name or f"{axis}_{bit}"):
        return lax.ppermute(x, axis, [(i, i ^ bit) for i in range(count)])


def pairings(count):
    both = [[(i, i + 1) for i in range(first, count - 1, 2)] for first in range(2)]
    return [p + [(b, a) for a, b in p] for p in both if p]


def faces_up(index, pairing):
    return (index + pairing) % 2 == 0


def meet(strips, axis, name):
    with jax.named_scope(name):
        return [
            lax.ppermute(strip, axis, pairs)
            for strip, pairs in zip(strips, pairings(lax.axis_size(axis)))
        ]


def low_high(index, received):
    if not received:
        return None, None
    first = received[0]
    second = received[1] if len(received) > 1 else jnp.zeros_like(first)
    odd = index % 2 == 1
    return jnp.where(odd, first, second), jnp.where(odd, second, first)


def side_rows(height):
    return round_up(MARGIN * (height + 2 * MARGIN), 16)


def emit_top(cells, outs, height, breadth):
    size = MARGIN * breadth
    for pairing, out in enumerate(outs):
        up = faces_up(lax.axis_index("section"), pairing)
        for lane in range(cells.shape[0]):
            out[:, lane * 128 : (lane + 1) * 128] = jnp.where(
                up, cells[lane, height * breadth - size :, :], cells[lane, :size, :]
            ).astype(BF16)


def sides_kernel(dims, n_top, cells, *refs):
    height, breadth = dims
    tops, (*outs, blocks) = refs[:n_top], refs[n_top:]
    size = MARGIN * breadth
    tall = height + 2 * MARGIN
    for lane in range(blocks.shape[0]):
        lanes = slice(lane * 128, (lane + 1) * 128)
        block = blocks.at[lane]
        low, high = low_high(lax.axis_index("section"), [top[:, lanes].astype(F32) for top in tops])
        block[:size, :] = jnp.zeros((size, 128), F32) if low is None else low
        block[size : size + height * breadth, :] = cells[:, lanes].astype(F32)
        block[size + height * breadth :, :] = jnp.zeros((size, 128), F32) if high is None else high
        for pairing, out in enumerate(outs):
            up = faces_up(lax.axis_index("row"), pairing)
            columns = [
                jnp.where(
                    up,
                    block[pl.ds(breadth - MARGIN + j, tall, stride=breadth), :],
                    block[pl.ds(j, tall, stride=breadth), :],
                )
                for j in range(MARGIN)
            ]
            spare = out.shape[0] - MARGIN * tall
            if spare:
                columns.append(jnp.zeros((spare, 128), F32))
            out[:, lanes] = jnp.concatenate(columns, axis=0).astype(BF16)


LEFT = 8


def padded_width(breadth):
    return round_up(LEFT + breadth + MARGIN, 8)


def fill_padded(pad, cells, tops, columns, height, breadth):
    width = padded_width(breadth)
    tall = height + 2 * MARGIN
    for lane in range(pad.shape[0]):
        block, lanes = pad.at[lane], slice(lane * 128, (lane + 1) * 128)
        for i in range(height):
            start = (MARGIN + i) * width + LEFT
            block[start : start + breadth, :] = cells[i * breadth : (i + 1) * breadth, lanes].astype(F32)
        low, high = low_high(lax.axis_index("section"), [top[:, lanes].astype(F32) for top in tops])
        for i in range(MARGIN):
            for row, strip in ((i, low), (MARGIN + height + i, high)):
                start = row * width + LEFT
                block[start : start + breadth, :] = (
                    jnp.zeros((breadth, 128), F32)
                    if strip is None
                    else strip[i * breadth : (i + 1) * breadth, :]
                )
        low, high = low_high(lax.axis_index("row"), [c[:, lanes].astype(F32) for c in columns])
        for j in range(MARGIN):
            for column, strip in ((LEFT - MARGIN + j, low), (LEFT + breadth + j, high)):
                block[pl.ds(column, tall, stride=width), :] = (
                    jnp.zeros((tall, 128), F32)
                    if strip is None
                    else strip[j * tall : (j + 1) * tall, :]
                )


def convolve(pad, shifted, taps, height, breadth, flip, store):
    width = padded_width(breadth)
    tall = height + 2 * MARGIN
    step = 4 if height % 4 == 0 else 1
    for lane in range(pad.shape[0]):
        lanes = slice(lane * 128, (lane + 1) * 128)
        for b in range(KERNEL):
            for i in range(tall):
                start = i * width + LEFT - MARGIN + b
                shifted[b, i * breadth : (i + 1) * breadth, :] = pad[lane, start : start + breadth, :]
        for top in range(0, height, step):
            totals = [jnp.zeros((breadth, 128), F32) for _ in range(step)]
            for b in range(KERNEL):
                rows = [
                    shifted[b, (top + i) * breadth : (top + i + 1) * breadth, :]
                    for i in range(step + 2 * MARGIN)
                ]
                for a in range(KERNEL):
                    p, q = (KERNEL - 1 - a, KERNEL - 1 - b) if flip else (a, b)
                    tap = taps[p, q, lanes][None, :]
                    totals = [total + rows[i + a] * tap for i, total in enumerate(totals)]
            total = jnp.concatenate(totals, axis=0)
            store(slice(top * breadth, (top + step) * breadth), lanes, total)


def split3(x):
    high = x.astype(BF16)
    left = x - high.astype(F32)
    mid = left.astype(BF16)
    return high, mid, (left - mid.astype(F32)).astype(BF16)


def message_rows(cells, channels):
    return 2 * cells + round_up(2 * (cells // channels) + 3, 16)


def forward_conv_kernel(dims, n_top, n_side, image, taps, gain, upstream, *refs):
    tops, columns, refs = refs[:n_top], refs[n_top : n_top + n_side], refs[n_top + n_side :]
    message, pad, shifted, mixed, tail = refs
    height, breadth = dims
    cells, channels = image.shape
    fill_padded(pad, image, tops, columns, height, breadth)

    def store(rows, lanes, total):
        mixed[rows, lanes] = total

    convolve(pad, shifted, taps, height, breadth, False, store)
    mean = jnp.sum(mixed[...], axis=1, keepdims=True) * (1.0 / channels)
    first = mean.astype(BF16).astype(F32)
    second = (mean - first).astype(BF16).astype(F32)
    message[:cells, :] = ((mixed[...] - first) - second).astype(BF16)
    tail[...] = jnp.zeros_like(tail)
    per = cells // channels
    for t, column in enumerate((first, second)):
        flat = jnp.broadcast_to(column, (cells, 128)).T
        for p in range(per):
            tail[t * per + p : t * per + p + 1, :] = flat[:1, p * channels : (p + 1) * channels]
    for t, part in enumerate(split3(gain[...])):
        tail[2 * per + t : 2 * per + t + 1, :] = part.astype(F32)
    message[cells : message.shape[0] - cells, :] = tail[...].astype(BF16)
    message[message.shape[0] - cells :, :] = upstream[...]


def mlp_kernel(in_slots, out_slots, n_col, *refs):
    messages, refs = refs[:n_col], refs[n_col:]
    n_in = sum(len(indices) for _, indices in in_slots)
    in_refs, refs = refs[:n_in], refs[n_in:]
    n_out = len(out_slots) * n_col
    out_refs, refs = refs[:n_out], refs[n_out:]
    outs, refs = refs[:n_col], refs[n_col:]
    hidden, normed, scaled, ups, gains, grads, act_grad = refs
    cells, channels = outs[0].shape
    up_at = messages[0].shape[0] - cells
    all_channels = n_col * channels
    per = cells // channels

    means = []
    for k, message in enumerate(messages):
        tail = message[cells:up_at, :].astype(F32)
        flat = tail[:per, :] + tail[per : 2 * per, :]
        row = jnp.concatenate([flat[p : p + 1, :] for p in range(per)], axis=1)
        means.append(jnp.broadcast_to(row, (128, cells)).T[:, :1])
        gains[k] = jnp.broadcast_to(sum(tail[2 * per + t : 2 * per + t + 1, :] for t in range(3)), gains.shape[1:])
        ups[k] = message[up_at:, :]
    centre = sum(means) * (1.0 / n_col)
    spread = jnp.zeros((cells, 1), F32)
    for k, message in enumerate(messages):
        centred = message[:cells, :].astype(F32) + (means[k] - centre)
        normed[k] = centred
        spread += jnp.sum(centred * centred, axis=1, keepdims=True)
    inv_std = lax.rsqrt(spread * (1.0 / all_channels) + EPSILON)
    for k in range(n_col):
        value = normed[k] * inv_std
        normed[k] = value
        scaled[k] = (value * gains[k][:1, :]).astype(BF16)
    share = act_grad.shape[2]
    tile = min(256, share)
    slots = [slot() for slot, _ in in_slots]
    places = []

    def w_in_columns(j, p, start, size):
        indices = in_slots[j][1]
        if len(indices) > 1:
            return in_refs[indices[p]][:, start : start + size]
        return in_refs[indices[0]][:, pl.ds(pl.multiple_of(places[p] + start, size), size)]

    for p, (part, blocks) in enumerate(out_slots):
        blocks = [block() for block in blocks]
        place = part() * share
        places.append(place)
        for start in range(0, share, tile):
            preact = sum(
                jnp.dot(scaled[slot], w_in_columns(j, p, start, tile), preferred_element_type=F32)
                for j, slot in enumerate(slots)
            )
            hidden_grad = sum(
                lax.dot_general(
                    ups[block],
                    out_refs[p * n_col + j][start : start + tile, :],
                    (((1,), (1,)), ((), ())),
                    preferred_element_type=F32,
                )
                for j, block in enumerate(blocks)
            )
            phi = 0.5 * (1.0 + lax.erf(preact * math.sqrt(0.5)))
            hidden[p, :, start : start + tile] = (preact * phi).astype(BF16)
            slope = phi + preact * jnp.exp(-0.5 * preact * preact) * (1.0 / math.sqrt(2.0 * math.pi))
            act_grad[p, :, start : start + tile] = (hidden_grad * slope).astype(BF16)
    first, second = jnp.zeros((cells, 1), F32), jnp.zeros((cells, 1), F32)
    for j, slot in enumerate(slots):
        grad = sum(
            lax.dot_general(
                act_grad[p], w_in_columns(j, p, 0, share), (((1,), (1,)), ((), ())), preferred_element_type=F32
            )
            for p in range(len(places))
        ) * gains[slot][:1, :]
        grads[slot] = grad
        first += jnp.sum(grad, axis=1, keepdims=True)
        second += jnp.sum(grad * normed[slot], axis=1, keepdims=True)
    first, second = first * (1.0 / all_channels), second * (1.0 / all_channels)
    for k in range(n_col):
        outs[k][...] = (inv_std * (grads[k] - first - normed[k] * second)).astype(BF16)


def branch_kernel(out_slots, n_col, hidden, *refs):
    n_out = len(out_slots) * n_col
    out_refs, (*outs, whole) = refs[:n_out], refs[n_out:]
    for j in range(n_col):
        whole[out_slots[0][1][j]()] = sum(
            jnp.dot(hidden[p], out_refs[p * n_col + j][...], preferred_element_type=F32)
            for p in range(len(out_slots))
        ).astype(BF16)
    for k in range(n_col):
        outs[k][...] = whole[k]


def grad_sum_kernel(dims, n_col, *refs):
    parts, (total, *outs, blocks) = refs[:n_col], refs[n_col:]
    for lane in range(blocks.shape[0]):
        lanes = slice(lane * 128, (lane + 1) * 128)
        blocks[lane] = sum(part[:, lanes].astype(F32) for part in parts)
        total[:, lanes] = blocks[lane]
    emit_top(blocks, outs, *dims)


def backward_conv_kernel(dims, n_top, n_side, n_terms, grad, taps, upstream, image, *refs):
    tops, columns, refs = refs[:n_top], refs[n_top : n_top + n_side], refs[n_top + n_side :]
    terms, (out, output, pad, shifted) = refs[:n_terms], refs[n_terms:]
    output[...] = (image[...].astype(F32) + sum(term[...].astype(F32) for term in terms)).astype(BF16)
    height, breadth = dims
    fill_padded(pad, grad, tops, columns, height, breadth)

    def store(rows, lanes, total):
        out[rows, lanes] = total + upstream[rows, lanes].astype(F32)

    convolve(pad, shifted, taps, height, breadth, True, store)


def call(name, vmem, kernel, out_shape, in_specs, scratch, flops=0, bytes_accessed=1 << 20, transcendentals=0):
    return pl.pallas_call(
        kernel,
        name=name,
        out_shape=out_shape,
        in_specs=in_specs,
        out_specs=jax.tree.map(lambda _: pl.BlockSpec(memory_space=pltpu.VMEM), out_shape),
        scratch_shapes=scratch,
        compiler_params=pltpu.CompilerParams(vmem_limit_bytes=vmem),
        cost_estimate=pl.CostEstimate(
            flops=flops, bytes_accessed=bytes_accessed, transcendentals=transcendentals
        ),
    )


IN_VMEM = pl.BlockSpec(memory_space=pltpu.VMEM)


def tie(x, *others):
    return lax.optimization_barrier((x, others))[0]


def exchangeable():
    n_sec, n_row, n_col = (lax.axis_size(a) for a in ("section", "row", "col"))
    return n_row == n_col and not n_row & (n_row - 1) and not n_sec & (n_sec - 1)


def far_rows(w_in, p, *others):
    share = w_in.shape[1] // lax.axis_size("section")
    mine = lax.dynamic_slice_in_dim(w_in, (lax.axis_index("section") ^ p) * share, share, 1)
    got = {(0, p): tie(mine, *others) if others else mine}
    for bit in bits_of(lax.axis_size("row"))[1:]:
        got |= {(r ^ bit, p): swap(x, "row", bit, f"w_in_row_{p}") for (r, p), x in got.items()}
    del got[0, p]
    return got


def weights_begin(w_in, w_out):
    n_sec, n_row, n_col = (lax.axis_size(a) for a in ("section", "row", "col"))
    if not exchangeable():
        return None, None, []
    share = w_in.shape[1] // n_sec
    mine_out = lax.dynamic_slice_in_dim(w_out, lax.axis_index("section") * share, share, 0)
    with jax.named_scope("w_out_transposed"):
        mine_out = lax.ppermute(
            mine_out,
            ("row", "col"),
            [(r * n_col + z, (z ^ (n_row // 2)) * n_col + r) for r in range(n_row) for z in range(n_col)],
        )
    early = far_rows(w_in, 0)
    return mine_out, early, [swap(w_in, "row", bit, "w_in_core") for bit in bits_of(n_row)[:1]]


def weights_far(mine_out, others):
    if not exchangeable():
        return None, []
    got = {(0, 0): tie(mine_out, others)}
    for bit in bits_of(lax.axis_size("row"))[1:]:
        got |= {(r ^ bit, s): swap(x, "row", bit, "w_out_row") for (r, s), x in got.items()}
    for bit in bits_of(lax.axis_size("section")):
        got |= {
            (0, s ^ bit): swap(x, "section", bit, "w_out_section") for (r, s), x in got.items() if r == 0
        }
    return got, list(got.values())


def weights_finish(w_in, w_out, got_out, got_in, core_in, rows_done, messages):
    n_sec, n_row, n_col = (lax.axis_size(a) for a in ("section", "row", "col"))
    channels, hidden = w_in.shape[0] * n_row // n_col, w_in.shape[1]
    if not exchangeable():
        order = jnp.arange(n_col) ^ lax.axis_index("col")
        whole_in = lax.all_gather(w_in, "row", axis=0, tiled=True)
        whole_in = whole_in.reshape(n_col, channels, hidden)[order].reshape(-1, hidden)
        whole_out = lax.all_gather(w_out, "row", axis=0, tiled=True)
        whole_out = lax.all_to_all(whole_out, "col", 0, 1, tiled=True)
        whole_out = whole_out.reshape(hidden, n_col, channels)[:, order].reshape(hidden, -1)
        fixed = [functools.partial(int, k) for k in range(n_col)]
        cut = [slice(k * channels, (k + 1) * channels) for k in range(n_col)]
        return [whole_in[c] for c in cut], [(f, [k]) for k, f in enumerate(fixed)], [whole_out[:, c] for c in cut], [(functools.partial(int, 0), fixed)]

    def block(row_bits):
        return lambda: (lax.axis_index("row") ^ row_bits) ^ lax.axis_index("col")

    def part(sec_bits):
        return lambda: lax.axis_index("section") ^ sec_bits

    core = bits_of(n_row)[:1]
    for bit in bits_of(n_sec):
        got_out |= {
            (r, s ^ bit): swap(x, "section", bit, "w_out_both") for (r, s), x in got_out.items() if r and s < bit
        }
    for p in range(1, n_sec):
        got_in |= far_rows(w_in, p, rows_done)
    got_in[0, None] = w_in
    for bit in core:
        got_in |= {
            (r ^ bit, s): core_in[0] if r == 0 else swap(x, "row", bit, f"w_in_core_{r}_{s}")
            for (r, s), x in got_in.items()
        }
        gate = swap(tie(got_out[0, 0], messages), "row", bit, "w_out_core_0_0")
        got_out |= {(bit, 0): gate} | {
            (r ^ bit, s): swap(tie(x, gate) if r and s else x, "row", bit, f"w_out_core_{r}_{s}")
            for (r, s), x in got_out.items()
            if r or s
        }
    keys = list(got_in)
    whole = [(block(r), [n]) for n, (r, p) in enumerate(keys) if p is None]
    cut = [(block(r), [keys.index((r, p)) for p in range(n_sec)]) for r, p in keys if p == 0]
    return (
        list(got_in.values()),
        whole + cut,
        [got_out[r, p] for p in range(n_sec) for r in range(n_row)],
        [(part(p), [block(r ^ (n_row // 2)) for r in range(n_row)]) for p in range(n_sec)],
    )


def local(image, conv_kernel, norm_gain, w_in, w_out, upstream):
    height, breadth, channels = image.shape
    dims = (height, breadth)
    cells = height * breadth
    n_sec, n_row, n_col = (lax.axis_size(a) for a in ("section", "row", "col"))
    all_channels, hidden = n_col * channels, w_in.shape[1]
    top = jax.ShapeDtypeStruct((MARGIN * breadth, channels), BF16)
    side = jax.ShapeDtypeStruct((side_rows(height), channels), BF16)
    n_top, n_side = len(pairings(n_sec)), len(pairings(n_row))
    padded = [
        pltpu.VMEM((channels // 128, (height + 2 * MARGIN) * padded_width(breadth), 128), F32),
        pltpu.VMEM((KERNEL, (height + 2 * MARGIN) * breadth, 128), F32),
    ]
    conv_cost = dict(flops=2 * KERNEL * KERNEL * cells * channels * 30)

    def columns_of(cell_values, tops, name):
        sent = call(
            name,
            4 * MIB,
            functools.partial(sides_kernel, dims, n_top),
            [side] * n_side,
            [IN_VMEM] * (1 + n_top),
            [pltpu.VMEM((channels // 128, (height + 2 * MARGIN) * breadth, 128), F32)],
        )(cell_values, *tops)
        return meet(sent, "row", name)

    def to_col(parts, name):
        with jax.named_scope(name):
            return [p if k == 0 else swap(p, "col", k) for k, p in enumerate(parts)]

    def gather_col(part, name, others):
        got = {0: part}
        with jax.named_scope(name):
            for bit in reversed(bits_of(n_col)):
                own = swap(part, "col", bit)
                got |= {k ^ bit: swap(tie(x, others, own), "col", bit) for k, x in got.items() if k}
                got[bit] = own
        return [got[k] for k in range(n_col)]

    def scatter_col(parts, name, others):
        terms = [[p] for p in parts]
        with jax.named_scope(name):
            for bit in bits_of(n_col):
                for k in range(bit, n_col, 2 * bit):
                    far, *more = terms[k]
                    if more:
                        more = tie(more, others)
                        far = sum((m.astype(F32) for m in more), far.astype(F32)).astype(BF16)
                    terms[k ^ bit].append(swap(far, "col", bit))
        return terms[0]

    flat_image = image.reshape(cells, channels)
    flat_up = upstream.reshape(cells, channels)
    mine_out, early_in, core_in = weights_begin(w_in, w_out)
    size = MARGIN * breadth
    sent = [
        lax.dynamic_slice_in_dim(
            flat_image, jnp.where(faces_up(lax.axis_index("section"), p), cells - size, 0), size, 0
        )
        for p in range(n_top)
    ]
    tops = meet(sent, "section", "image_rows")
    columns = columns_of(flat_image, tops, "image_columns")
    rows = message_rows(cells, channels)
    message = call(
        "forward_conv",
        8 * MIB,
        functools.partial(forward_conv_kernel, dims, n_top, n_side),
        jax.ShapeDtypeStruct((rows, channels), BF16),
        [IN_VMEM] * (4 + n_top + n_side),
        padded + [pltpu.VMEM((cells, channels), F32), pltpu.VMEM((rows - 2 * cells, channels), F32)],
        **conv_cost,
    )(tie(flat_image, core_in), conv_kernel, norm_gain.reshape(1, channels), flat_up, *tops, *columns)

    early = [] if early_in is None else list(early_in.values())
    got_out, rows_done = weights_far(mine_out, [message, early])
    messages = gather_col(message, "features", rows_done)
    in_refs, in_pieces, out_refs, out_pieces = weights_finish(
        w_in, w_out, got_out, early_in, core_in, rows_done, messages
    )

    product = 2 * cells * all_channels * hidden
    part = jax.ShapeDtypeStruct((cells, channels), BF16)
    act_shape = (len(out_pieces), cells, hidden // len(out_pieces))
    *grads, act = call(
        "mlp",
        24 * MIB,
        functools.partial(mlp_kernel, in_pieces, out_pieces, n_col),
        [part] * n_col + [jax.ShapeDtypeStruct(act_shape, BF16)],
        [IN_VMEM] * (n_col + len(in_refs) + len(out_refs)),
        [
            pltpu.VMEM((n_col, cells, channels), F32),
            pltpu.VMEM((n_col, cells, channels), BF16),
            pltpu.VMEM((n_col, cells, channels), BF16),
            pltpu.VMEM((n_col, 8, channels), F32),
            pltpu.VMEM((n_col, cells, channels), F32),
            pltpu.VMEM(act_shape, BF16),
        ],
        flops=3 * product,
        transcendentals=2 * cells * hidden,
    )(*messages, *in_refs, *out_refs)
    grads = to_col(grads, "grad_sums")
    act = tie(act, grads[2])
    branches = call(
        "branch",
        12 * MIB,
        functools.partial(branch_kernel, out_pieces, n_col),
        [part] * n_col,
        [IN_VMEM] * (1 + len(out_refs)),
        [pltpu.VMEM((n_col, cells, channels), BF16)],
        flops=product,
    )(act, *out_refs)
    mixed_grad, *sent = call(
        "grad_sum",
        4 * MIB,
        functools.partial(grad_sum_kernel, dims, n_col),
        [jax.ShapeDtypeStruct((cells, channels), F32)] + [top] * n_top,
        [IN_VMEM] * n_col,
        [pltpu.VMEM((channels // 128, cells, 128), F32)],
    )(*grads)
    tops = meet(sent, "section", "grad_rows")
    branches = scatter_col(branches, "branch_sums", tops)
    columns = columns_of(mixed_grad, tops, "grad_columns")
    image_grad, output = call(
        "backward_conv",
        8 * MIB,
        functools.partial(backward_conv_kernel, dims, n_top, n_side, len(branches)),
        [jax.ShapeDtypeStruct((cells, channels), F32), part],
        [IN_VMEM] * (4 + n_top + n_side + len(branches)),
        padded,
        **conv_cost,
    )(mixed_grad, conv_kernel, flat_up, flat_image, *tops, *columns, *branches)
    return output.reshape(image.shape), image_grad.reshape(image.shape)


def solution(mesh):
    in_specs = (
        P("section", "row", "col"),
        P(None, None, "col"),
        P("col"),
        P("row", "col"),
        P("row", "col"),
        P("section", "row", "col"),
    )
    out_specs = (P("section", "row", "col"), P("section", "row", "col"))
    return jax.shard_map(local, mesh=mesh, in_specs=in_specs, out_specs=out_specs, check_vma=False)
```

```python
import functools
import math

import jax
import jax.numpy as jnp
from jax import lax
from jax.experimental import pallas as pl
from jax.experimental.pallas import tpu as pltpu
from jax.sharding import PartitionSpec as P

KERNEL = 7
MARGIN = KERNEL // 2
EPSILON = 1e-06
BF16, F32 = jnp.bfloat16, jnp.float32
MIB = 1024 * 1024


def round_up(value, to):
    return -(-value // to) * to


def bits_of(count):
    return [1 << b for b in range(count.bit_length() - 1)]


def swap(x, axis, bit, name=None):
    count = lax.axis_size(axis)
    with jax.named_scope(name or f"{axis}_{bit}"):
        return lax.ppermute(x, axis, [(i, i ^ bit) for i in range(count)])


def pairings(count):
    both = [[(i, i + 1) for i in range(first, count - 1, 2)] for first in range(2)]
    return [p + [(b, a) for a, b in p] for p in both if p]


def faces_up(index, pairing):
    return (index + pairing) % 2 == 0


def meet(strips, axis, name):
    with jax.named_scope(name):
        return [
            lax.ppermute(strip, axis, pairs)
            for strip, pairs in zip(strips, pairings(lax.axis_size(axis)))
        ]


def low_high(index, received):
    if not received:
        return None, None
    first = received[0]
    second = received[1] if len(received) > 1 else jnp.zeros_like(first)
    odd = index % 2 == 1
    return jnp.where(odd, first, second), jnp.where(odd, second, first)


def side_rows(height):
    return round_up(MARGIN * (height + 2 * MARGIN), 16)


def emit_top(cells, outs, height, breadth):
    size = MARGIN * breadth
    for pairing, out in enumerate(outs):
        up = faces_up(lax.axis_index("section"), pairing)
        for lane in range(cells.shape[0]):
            out[:, lane * 128 : (lane + 1) * 128] = jnp.where(
                up, cells[lane, height * breadth - size :, :], cells[lane, :size, :]
            ).astype(BF16)


def sides_kernel(dims, n_top, cells, *refs):
    height, breadth = dims
    tops, (*outs, blocks) = refs[:n_top], refs[n_top:]
    size = MARGIN * breadth
    tall = height + 2 * MARGIN
    for lane in range(blocks.shape[0]):
        lanes = slice(lane * 128, (lane + 1) * 128)
        block = blocks.at[lane]
        low, high = low_high(lax.axis_index("section"), [top[:, lanes].astype(F32) for top in tops])
        block[:size, :] = jnp.zeros((size, 128), F32) if low is None else low
        block[size : size + height * breadth, :] = cells[:, lanes].astype(F32)
        block[size + height * breadth :, :] = jnp.zeros((size, 128), F32) if high is None else high
        for pairing, out in enumerate(outs):
            up = faces_up(lax.axis_index("row"), pairing)
            columns = [
                jnp.where(
                    up,
                    block[pl.ds(breadth - MARGIN + j, tall, stride=breadth), :],
                    block[pl.ds(j, tall, stride=breadth), :],
                )
                for j in range(MARGIN)
            ]
            spare = out.shape[0] - MARGIN * tall
            if spare:
                columns.append(jnp.zeros((spare, 128), F32))
            out[:, lanes] = jnp.concatenate(columns, axis=0).astype(BF16)


LEFT = 8


def padded_width(breadth):
    return round_up(LEFT + breadth + MARGIN, 8)


def fill_padded(pad, cells, tops, columns, height, breadth):
    width = padded_width(breadth)
    tall = height + 2 * MARGIN
    for lane in range(pad.shape[0]):
        block, lanes = pad.at[lane], slice(lane * 128, (lane + 1) * 128)
        for i in range(height):
            start = (MARGIN + i) * width + LEFT
            block[start : start + breadth, :] = cells[i * breadth : (i + 1) * breadth, lanes].astype(F32)
        low, high = low_high(lax.axis_index("section"), [top[:, lanes].astype(F32) for top in tops])
        for i in range(MARGIN):
            for row, strip in ((i, low), (MARGIN + height + i, high)):
                start = row * width + LEFT
                block[start : start + breadth, :] = (
                    jnp.zeros((breadth, 128), F32)
                    if strip is None
                    else strip[i * breadth : (i + 1) * breadth, :]
                )
        low, high = low_high(lax.axis_index("row"), [c[:, lanes].astype(F32) for c in columns])
        for j in range(MARGIN):
            for column, strip in ((LEFT - MARGIN + j, low), (LEFT + breadth + j, high)):
                block[pl.ds(column, tall, stride=width), :] = (
                    jnp.zeros((tall, 128), F32)
                    if strip is None
                    else strip[j * tall : (j + 1) * tall, :]
                )


def convolve(pad, shifted, taps, height, breadth, flip, store):
    width = padded_width(breadth)
    tall = height + 2 * MARGIN
    step = 4 if height % 4 == 0 else 1
    for lane in range(pad.shape[0]):
        lanes = slice(lane * 128, (lane + 1) * 128)
        for b in range(KERNEL):
            for i in range(tall):
                start = i * width + LEFT - MARGIN + b
                shifted[b, i * breadth : (i + 1) * breadth, :] = pad[lane, start : start + breadth, :]
        for top in range(0, height, step):
            totals = [jnp.zeros((breadth, 128), F32) for _ in range(step)]
            for b in range(KERNEL):
                rows = [
                    shifted[b, (top + i) * breadth : (top + i + 1) * breadth, :]
                    for i in range(step + 2 * MARGIN)
                ]
                for a in range(KERNEL):
                    p, q = (KERNEL - 1 - a, KERNEL - 1 - b) if flip else (a, b)
                    tap = taps[p, q, lanes][None, :]
                    totals = [total + rows[i + a] * tap for i, total in enumerate(totals)]
            total = jnp.concatenate(totals, axis=0)
            store(slice(top * breadth, (top + step) * breadth), lanes, total)


def split3(x):
    high = x.astype(BF16)
    left = x - high.astype(F32)
    mid = left.astype(BF16)
    return high, mid, (left - mid.astype(F32)).astype(BF16)


def message_rows(cells, channels):
    return 2 * cells + round_up(2 * (cells // channels) + 3, 16)


def forward_conv_kernel(dims, n_top, n_side, image, taps, gain, upstream, *refs):
    tops, columns, refs = refs[:n_top], refs[n_top : n_top + n_side], refs[n_top + n_side :]
    message, pad, shifted, mixed, tail, gain_here, sem = refs
    gain_copy = pltpu.make_async_copy(gain, gain_here, sem)
    gain_copy.start()
    height, breadth = dims
    cells, channels = image.shape
    fill_padded(pad, image, tops, columns, height, breadth)

    def store(rows, lanes, total):
        mixed[rows, lanes] = total

    convolve(pad, shifted, taps, height, breadth, False, store)
    mean = jnp.sum(mixed[...], axis=1, keepdims=True) * (1.0 / channels)
    first = mean.astype(BF16).astype(F32)
    second = (mean - first).astype(BF16).astype(F32)
    message[:cells, :] = ((mixed[...] - first) - second).astype(BF16)
    tail[...] = jnp.zeros_like(tail)
    per = cells // channels
    for t, column in enumerate((first, second)):
        flat = jnp.broadcast_to(column, (cells, 128)).T
        for p in range(per):
            tail[t * per + p : t * per + p + 1, :] = flat[:1, p * channels : (p + 1) * channels]
    gain_copy.wait()
    for t, part in enumerate(split3(gain_here[...])):
        tail[2 * per + t : 2 * per + t + 1, :] = part.astype(F32)
    message[cells : message.shape[0] - cells, :] = tail[...].astype(BF16)
    message[message.shape[0] - cells :, :] = upstream[...]


def mlp_kernel(in_slots, out_slots, n_col, *refs):
    messages, refs = refs[:n_col], refs[n_col:]
    n_in = sum(len(indices) for _, indices in in_slots)
    in_refs, refs = refs[:n_in], refs[n_in:]
    n_out = len(out_slots) * n_col
    out_refs, refs = refs[:n_out], refs[n_out:]
    outs, refs = refs[:n_col], refs[n_col:]
    hidden, normed, scaled, ups, gains, grads, act_grad = refs
    cells, channels = outs[0].shape
    up_at = messages[0].shape[0] - cells
    all_channels = n_col * channels
    per = cells // channels

    means = []
    for k, message in enumerate(messages):
        tail = message[cells:up_at, :].astype(F32)
        flat = tail[:per, :] + tail[per : 2 * per, :]
        row = jnp.concatenate([flat[p : p + 1, :] for p in range(per)], axis=1)
        means.append(jnp.broadcast_to(row, (128, cells)).T[:, :1])
        gains[k] = jnp.broadcast_to(sum(tail[2 * per + t : 2 * per + t + 1, :] for t in range(3)), gains.shape[1:])
        ups[k] = message[up_at:, :]
    centre = sum(means) * (1.0 / n_col)
    spread = jnp.zeros((cells, 1), F32)
    for k, message in enumerate(messages):
        centred = message[:cells, :].astype(F32) + (means[k] - centre)
        normed[k] = centred
        spread += jnp.sum(centred * centred, axis=1, keepdims=True)
    inv_std = lax.rsqrt(spread * (1.0 / all_channels) + EPSILON)
    for k in range(n_col):
        value = normed[k] * inv_std
        normed[k] = value
        scaled[k] = (value * gains[k][:1, :]).astype(BF16)
    share = act_grad.shape[2]
    tile = min(512, share)
    slots = [slot() for slot, _ in in_slots]
    places = []

    def w_in_columns(j, p, start, size):
        indices = in_slots[j][1]
        if len(indices) > 1:
            return in_refs[indices[p]][:, start : start + size]
        return in_refs[indices[0]][:, pl.ds(pl.multiple_of(places[p] + start, size), size)]

    for p, (part, blocks) in enumerate(out_slots):
        blocks = [block() for block in blocks]
        place = part() * share
        places.append(place)
        for start in range(0, share, tile):
            preact = sum(
                jnp.dot(scaled[slot], w_in_columns(j, p, start, tile), preferred_element_type=F32)
                for j, slot in enumerate(slots)
            )
            hidden_grad = sum(
                lax.dot_general(
                    ups[block],
                    out_refs[p * n_col + j][start : start + tile, :],
                    (((1,), (1,)), ((), ())),
                    preferred_element_type=F32,
                )
                for j, block in enumerate(blocks)
            )
            phi = 0.5 * (1.0 + lax.erf(preact * math.sqrt(0.5)))
            hidden[p, :, start : start + tile] = (preact * phi).astype(BF16)
            slope = phi + preact * jnp.exp(-0.5 * preact * preact) * (1.0 / math.sqrt(2.0 * math.pi))
            act_grad[p, :, start : start + tile] = (hidden_grad * slope).astype(BF16)
    first, second = jnp.zeros((cells, 1), F32), jnp.zeros((cells, 1), F32)
    for j, slot in enumerate(slots):
        grad = sum(
            lax.dot_general(
                act_grad[p], w_in_columns(j, p, 0, share), (((1,), (1,)), ((), ())), preferred_element_type=F32
            )
            for p in range(len(places))
        ) * gains[slot][:1, :]
        grads[slot] = grad
        first += jnp.sum(grad, axis=1, keepdims=True)
        second += jnp.sum(grad * normed[slot], axis=1, keepdims=True)
    first, second = first * (1.0 / all_channels), second * (1.0 / all_channels)
    for k in range(n_col):
        outs[k][...] = (inv_std * (grads[k] - first - normed[k] * second)).astype(BF16)


def branch_kernel(out_slots, n_col, hidden, *refs):
    n_out = len(out_slots) * n_col
    out_refs, (*outs, whole) = refs[:n_out], refs[n_out:]
    for j in range(n_col):
        whole[out_slots[0][1][j]()] = sum(
            jnp.dot(hidden[p], out_refs[p * n_col + j][...], preferred_element_type=F32)
            for p in range(len(out_slots))
        ).astype(BF16)
    for k in range(n_col):
        outs[k][...] = whole[k]


def grad_sum_kernel(dims, n_col, *refs):
    parts, (total, *outs, blocks) = refs[:n_col], refs[n_col:]
    for lane in range(blocks.shape[0]):
        lanes = slice(lane * 128, (lane + 1) * 128)
        blocks[lane] = sum(part[:, lanes].astype(F32) for part in parts)
        total[:, lanes] = blocks[lane]
    emit_top(blocks, outs, *dims)


def backward_conv_kernel(dims, n_top, n_side, n_terms, grad, taps, upstream, image, *refs):
    tops, columns, refs = refs[:n_top], refs[n_top : n_top + n_side], refs[n_top + n_side :]
    terms, (out, output, pad, shifted) = refs[:n_terms], refs[n_terms:]
    output[...] = (image[...].astype(F32) + sum(term[...].astype(F32) for term in terms)).astype(BF16)
    height, breadth = dims
    fill_padded(pad, grad, tops, columns, height, breadth)

    def store(rows, lanes, total):
        out[rows, lanes] = total + upstream[rows, lanes].astype(F32)

    convolve(pad, shifted, taps, height, breadth, True, store)


def call(name, vmem, kernel, out_shape, in_specs, scratch, flops=0, bytes_accessed=1 << 20, transcendentals=0):
    return pl.pallas_call(
        kernel,
        name=name,
        out_shape=out_shape,
        in_specs=in_specs,
        out_specs=jax.tree.map(lambda _: pl.BlockSpec(memory_space=pltpu.VMEM), out_shape),
        scratch_shapes=scratch,
        compiler_params=pltpu.CompilerParams(vmem_limit_bytes=vmem),
        cost_estimate=pl.CostEstimate(
            flops=flops, bytes_accessed=bytes_accessed, transcendentals=transcendentals
        ),
    )


IN_VMEM = pl.BlockSpec(memory_space=pltpu.VMEM)
IN_HBM = pl.BlockSpec(memory_space=pltpu.HBM)


def tie(x, *others):
    return lax.optimization_barrier((x, others))[0]


def exchangeable():
    n_sec, n_row, n_col = (lax.axis_size(a) for a in ("section", "row", "col"))
    return n_row == n_col and not n_row & (n_row - 1) and not n_sec & (n_sec - 1)


def far_rows(w_in, p, *others):
    share = w_in.shape[1] // lax.axis_size("section")
    mine = lax.dynamic_slice_in_dim(w_in, (lax.axis_index("section") ^ p) * share, share, 1)
    got = {(0, p): tie(mine, *others) if others else mine}
    for bit in bits_of(lax.axis_size("row"))[1:]:
        got |= {(r ^ bit, p): swap(x, "row", bit, f"w_in_row_{p}") for (r, p), x in got.items()}
    del got[0, p]
    return got


def weights_begin(w_in, w_out):
    n_sec, n_row, n_col = (lax.axis_size(a) for a in ("section", "row", "col"))
    if not exchangeable():
        return None, None, []
    share = w_in.shape[1] // n_sec
    mine_out = lax.dynamic_slice_in_dim(w_out, lax.axis_index("section") * share, share, 0)
    with jax.named_scope("w_out_transposed"):
        mine_out = lax.ppermute(
            mine_out,
            ("row", "col"),
            [(r * n_col + z, (z ^ (n_row // 2)) * n_col + r) for r in range(n_row) for z in range(n_col)],
        )
    early = far_rows(w_in, 0)
    return mine_out, early, [swap(w_in, "row", bit, "w_in_core") for bit in bits_of(n_row)[:1]]


def weights_far(mine_out, others):
    if not exchangeable():
        return None, []
    got = {(0, 0): tie(mine_out, others)}
    for bit in bits_of(lax.axis_size("row"))[1:]:
        got |= {(r ^ bit, s): swap(x, "row", bit, "w_out_row") for (r, s), x in got.items()}
    for bit in bits_of(lax.axis_size("section")):
        got |= {
            (0, s ^ bit): swap(x, "section", bit, "w_out_section") for (r, s), x in got.items() if r == 0
        }
    return got, list(got.values())


def weights_finish(w_in, w_out, got_out, got_in, core_in, rows_done, messages):
    n_sec, n_row, n_col = (lax.axis_size(a) for a in ("section", "row", "col"))
    channels, hidden = w_in.shape[0] * n_row // n_col, w_in.shape[1]
    if not exchangeable():
        order = jnp.arange(n_col) ^ lax.axis_index("col")
        whole_in = lax.all_gather(w_in, "row", axis=0, tiled=True)
        whole_in = whole_in.reshape(n_col, channels, hidden)[order].reshape(-1, hidden)
        whole_out = lax.all_gather(w_out, "row", axis=0, tiled=True)
        whole_out = lax.all_to_all(whole_out, "col", 0, 1, tiled=True)
        whole_out = whole_out.reshape(hidden, n_col, channels)[:, order].reshape(hidden, -1)
        fixed = [functools.partial(int, k) for k in range(n_col)]
        cut = [slice(k * channels, (k + 1) * channels) for k in range(n_col)]
        return [whole_in[c] for c in cut], [(f, [k]) for k, f in enumerate(fixed)], [whole_out[:, c] for c in cut], [(functools.partial(int, 0), fixed)]

    def block(row_bits):
        return lambda: (lax.axis_index("row") ^ row_bits) ^ lax.axis_index("col")

    def part(sec_bits):
        return lambda: lax.axis_index("section") ^ sec_bits

    core = bits_of(n_row)[:1]
    for bit in bits_of(n_sec):
        got_out |= {
            (r, s ^ bit): swap(x, "section", bit, "w_out_both") for (r, s), x in got_out.items() if r and s < bit
        }
    for p in range(1, n_sec):
        got_in |= far_rows(w_in, p, rows_done)
    got_in[0, None] = w_in
    for bit in core:
        got_in |= {
            (r ^ bit, s): core_in[0] if r == 0 else swap(x, "row", bit, f"w_in_core_{r}_{s}")
            for (r, s), x in got_in.items()
        }
        got_out |= {
            (r ^ bit, s): swap(tie(x, messages) if r and s else x, "row", bit, f"w_out_core_{r}_{s}")
            for (r, s), x in got_out.items()
        }
    keys = list(got_in)
    whole = [(block(r), [n]) for n, (r, p) in enumerate(keys) if p is None]
    cut = [(block(r), [keys.index((r, p)) for p in range(n_sec)]) for r, p in keys if p == 0]
    return (
        list(got_in.values()),
        whole + cut,
        [got_out[r, p] for p in range(n_sec) for r in range(n_row)],
        [(part(p), [block(r ^ (n_row // 2)) for r in range(n_row)]) for p in range(n_sec)],
    )


def local(image, conv_kernel, norm_gain, w_in, w_out, upstream):
    height, breadth, channels = image.shape
    dims = (height, breadth)
    cells = height * breadth
    n_sec, n_row, n_col = (lax.axis_size(a) for a in ("section", "row", "col"))
    all_channels, hidden = n_col * channels, w_in.shape[1]
    top = jax.ShapeDtypeStruct((MARGIN * breadth, channels), BF16)
    side = jax.ShapeDtypeStruct((side_rows(height), channels), BF16)
    n_top, n_side = len(pairings(n_sec)), len(pairings(n_row))
    padded = [
        pltpu.VMEM((channels // 128, (height + 2 * MARGIN) * padded_width(breadth), 128), F32),
        pltpu.VMEM((KERNEL, (height + 2 * MARGIN) * breadth, 128), F32),
    ]
    conv_cost = dict(flops=2 * KERNEL * KERNEL * cells * channels * 30)

    def columns_of(cell_values, tops, name):
        sent = call(
            name,
            4 * MIB,
            functools.partial(sides_kernel, dims, n_top),
            [side] * n_side,
            [IN_VMEM] * (1 + n_top),
            [pltpu.VMEM((channels // 128, (height + 2 * MARGIN) * breadth, 128), F32)],
        )(cell_values, *tops)
        return meet(sent, "row", name)

    def to_col(parts, name):
        with jax.named_scope(name):
            return [p if k == 0 else swap(p, "col", k) for k, p in enumerate(parts)]

    def gather_col(part, name, others):
        got = {0: part}
        with jax.named_scope(name):
            for bit in reversed(bits_of(n_col)):
                own = swap(part, "col", bit)
                got |= {k ^ bit: swap(tie(x, others, own), "col", bit) for k, x in got.items() if k}
                got[bit] = own
        return [got[k] for k in range(n_col)]

    def scatter_col(parts, name, others):
        terms = [[p] for p in parts]
        with jax.named_scope(name):
            for bit in bits_of(n_col):
                for k in range(bit, n_col, 2 * bit):
                    far, *more = terms[k]
                    if more:
                        more = tie(more, others)
                        far = sum((m.astype(F32) for m in more), far.astype(F32)).astype(BF16)
                    terms[k ^ bit].append(swap(far, "col", bit))
        return terms[0]

    flat_image = image.reshape(cells, channels)
    flat_up = upstream.reshape(cells, channels)
    mine_out, early_in, core_in = weights_begin(w_in, w_out)
    size = MARGIN * breadth
    sent = [
        lax.dynamic_slice_in_dim(
            flat_image, jnp.where(faces_up(lax.axis_index("section"), p), cells - size, 0), size, 0
        )
        for p in range(n_top)
    ]
    tops = meet(sent, "section", "image_rows")
    columns = columns_of(flat_image, tops, "image_columns")
    rows = message_rows(cells, channels)
    message = call(
        "forward_conv",
        8 * MIB,
        functools.partial(forward_conv_kernel, dims, n_top, n_side),
        jax.ShapeDtypeStruct((rows, channels), BF16),
        [IN_VMEM] * 2 + [IN_HBM] + [IN_VMEM] * (1 + n_top + n_side),
        padded + [pltpu.VMEM((cells, channels), F32), pltpu.VMEM((rows - 2 * cells, channels), F32)]
        + [pltpu.VMEM((1, channels), F32), pltpu.SemaphoreType.DMA],
        **conv_cost,
    )(tie(flat_image, core_in), conv_kernel, norm_gain.reshape(1, channels), flat_up, *tops, *columns)

    early = [] if early_in is None else list(early_in.values())
    got_out, rows_done = weights_far(mine_out, [message, early])
    messages = gather_col(message, "features", rows_done)
    in_refs, in_pieces, out_refs, out_pieces = weights_finish(
        w_in, w_out, got_out, early_in, core_in, rows_done, messages
    )

    product = 2 * cells * all_channels * hidden
    part = jax.ShapeDtypeStruct((cells, channels), BF16)
    act_shape = (len(out_pieces), cells, hidden // len(out_pieces))
    *grads, act = call(
        "mlp",
        24 * MIB,
        functools.partial(mlp_kernel, in_pieces, out_pieces, n_col),
        [part] * n_col + [jax.ShapeDtypeStruct(act_shape, BF16)],
        [IN_VMEM] * (n_col + len(in_refs) + len(out_refs)),
        [
            pltpu.VMEM((n_col, cells, channels), F32),
            pltpu.VMEM((n_col, cells, channels), BF16),
            pltpu.VMEM((n_col, cells, channels), BF16),
            pltpu.VMEM((n_col, 8, channels), F32),
            pltpu.VMEM((n_col, cells, channels), F32),
            pltpu.VMEM(act_shape, BF16),
        ],
        flops=3 * product,
        transcendentals=2 * cells * hidden,
    )(*messages, *in_refs, *out_refs)
    grads = to_col(grads, "grad_sums")
    act = tie(act, grads[2])
    branches = call(
        "branch",
        12 * MIB,
        functools.partial(branch_kernel, out_pieces, n_col),
        [part] * n_col,
        [IN_VMEM] * (1 + len(out_refs)),
        [pltpu.VMEM((n_col, cells, channels), BF16)],
        flops=product,
    )(act, *out_refs)
    mixed_grad, *sent = call(
        "grad_sum",
        4 * MIB,
        functools.partial(grad_sum_kernel, dims, n_col),
        [jax.ShapeDtypeStruct((cells, channels), F32)] + [top] * n_top,
        [IN_VMEM] * n_col,
        [pltpu.VMEM((channels // 128, cells, 128), F32)],
    )(*grads)
    tops = meet(sent, "section", "grad_rows")
    branches = scatter_col(branches, "branch_sums", tops)
    columns = columns_of(mixed_grad, tops, "grad_columns")
    image_grad, output = call(
        "backward_conv",
        8 * MIB,
        functools.partial(backward_conv_kernel, dims, n_top, n_side, len(branches)),
        [jax.ShapeDtypeStruct((cells, channels), F32), part],
        [IN_VMEM] * (4 + n_top + n_side + len(branches)),
        padded,
        **conv_cost,
    )(mixed_grad, conv_kernel, flat_up, flat_image, *tops, *columns, *branches)
    return output.reshape(image.shape), image_grad.reshape(image.shape)


def solution(mesh):
    in_specs = (
        P("section", "row", "col"),
        P(None, None, "col"),
        P("col"),
        P("row", "col"),
        P("row", "col"),
        P("section", "row", "col"),
    )
    out_specs = (P("section", "row", "col"), P("section", "row", "col"))
    return jax.shard_map(local, mesh=mesh, in_specs=in_specs, out_specs=out_specs, check_vma=False)
```
